128 devices in a mesh: group: 4 (over x_hi, core), expert: 32 (over z, y, x_lo).
Axes of the slice: x: 4 (x_hi: 2, x_lo: 2; x = x_hi * 2 + x_lo), y: 4, z: 4, core: 2. Of those that a mesh axis runs over, the one named last changes fastest.
Arguments:
- hidden_rows: bfloat16 [16384, 7168], P(('group', 'expert')), may hold values from -6 to 6
- embed_rows: bfloat16 [16384, 7168], P(('group', 'expert')), may hold values from -6 to 6
- gain_hidden: float32 [7168], replicated, may hold values from 0.1 to 1.9
- gain_embed: float32 [7168], replicated, may hold values from 0.1 to 1.9
- main_route: int32 [16384, 8], P(('group', 'expert')), may hold values from 0 to 255, as said below
- main_gates: float32 [16384, 8], P(('group', 'expert')), may hold values from 0.05 to 1
- draft_route: int32 [16384, 8], P(('group', 'expert')), may hold values from 0 to 255, as said below
- draft_gates: float32 [16384, 8], P(('group', 'expert')), may hold values from 0.05 to 1
- draft_cotangent: bfloat16 [16384, 7168], P(('group', 'expert')), may hold values from -6 to 6
- expert_in: bfloat16 [128, 7168, 384], P(('group', 'expert')), may hold values from -0.0625 to 0.0625
- expert_out: bfloat16 [128, 192, 7168], P(('group', 'expert')), may hold values from -0.15625 to 0.15625
Outputs:
- hidden_grad: bfloat16 [16384, 7168], P(('group', 'expert'))
- embed_grad: bfloat16 [16384, 7168], P(('group', 'expert'))
- in_grad: bfloat16 [128, 7168, 384], P(('group', 'expert'))
- out_grad: bfloat16 [128, 192, 7168], P(('group', 'expert'))
The draws below stay inside these ranges and needn't reach their ends.
Inputs may be any that keep to these rules, and one draw needn't show every extreme that they name: `main_route`: each row names 8 different experts. `draft_route`: each row names 8 different experts.
All inputs are finite; a program needn't handle non-finite values.
Results may differ from the reference program's by a relative error of at most 0.0068.
Values may be sent and summed in bfloat16 or wider, within the bound.
No kernel may reach another device: no remote copies, remote signals or barrier semaphores. Data moves between devices by JAX's collectives and lax.ppermute only.
A program may use at most 128 MiB of HBM per device.

```python
import math
import jax
import jax.numpy as jnp
from jax import lax

D = 7168
E_ALL = 256
FFE = 1536
TOPK = 8
SHARDS = 8
TOK_DEV = 128
CAP = 2
FS = 192
EXPG = 4
MAIN_EXP = 12
TOKENS = 16384
N_GROUP = 4
N_EXPERT = 32


def routed(key, window):
    scores = jax.random.randint(key, (TOKENS, E_ALL), 0, 1048576, dtype=jnp.int32)
    lowered = jax.random.randint(jax.random.fold_in(key, 1), (E_ALL,), 8192, 16384, dtype=jnp.int32)
    labels = jnp.arange(E_ALL, dtype=jnp.int32)
    scores = scores - jnp.where(labels < window, lowered, 0)
    scores = scores * E_ALL + labels
    values_top, picked = lax.top_k(scores, TOPK)
    return picked.astype(jnp.int32)


def draw_main_route(key, part):
    key = jax.random.fold_in(key, 7)
    return routed(key, MAIN_EXP)


def draw_draft_route(key, part):
    key = jax.random.fold_in(key, 9)
    return routed(key, EXPG)


def steps_of(own_key, extent, cuts, smallest, top_value):
    gain, own = 1.0, jax.random.fold_in(own_key, 6)
    for dim, blocks in cuts:
        draws = jnp.exp(jax.random.uniform(jax.random.fold_in(own, dim), (blocks,), jnp.float32, smallest / len(cuts), top_value / len(cuts)))
        gain = gain * jnp.repeat(draws, extent[dim] // blocks).reshape([-1 if axis == dim else 1 for axis in range(len(extent))])
    return gain


def gaussian(rng, dims, scale, most, shards=(), held_as=jnp.bfloat16):
    array = scale * jax.random.normal(rng, dims, jnp.float32)
    if shards:
        array = array * steps_of(rng, dims, shards, -0.22, 0.18)
    return jnp.clip(array, -most, most).astype(held_as)


def setup_inputs(seed: int = 0) -> dict:
    streams_of = jax.random.split(jax.random.key(seed), 12)
    return {
        "hidden_rows": gaussian(streams_of[0], (TOKENS, D), 1.0, 6.0, ((0, 128),)),
        "embed_rows": gaussian(streams_of[1], (TOKENS, D), 1.0, 6.0, ((0, 128),)),
        "gain_hidden": jnp.clip(1.0 + 0.18 * jax.random.normal(streams_of[2], (D,), jnp.float32), 0.1, 1.9),
        "gain_embed": jnp.clip(1.0 + 0.18 * jax.random.normal(streams_of[3], (D,), jnp.float32), 0.1, 1.9),
        "main_route": draw_main_route(jax.random.fold_in(streams_of[11], 71), 0),
        "main_gates": jnp.clip(jnp.exp(math.log(1.0) - 2.9957323 * jax.random.uniform(streams_of[5], (TOKENS, TOPK), jnp.float32) ** steps_of(streams_of[5], (TOKENS, TOPK), ((0, 128),), -0.2, 0.2)), 0.05, 1.0),
        "draft_route": draw_draft_route(jax.random.fold_in(streams_of[11], 71), 0),
        "draft_gates": jnp.clip(jnp.exp(math.log(1.0) - 2.9957323 * jax.random.uniform(streams_of[7], (TOKENS, TOPK), jnp.float32) ** steps_of(streams_of[7], (TOKENS, TOPK), ((0, 128),), -0.2, 0.2)), 0.05, 1.0),
        "draft_cotangent": gaussian(streams_of[8], (TOKENS, D), 1.0, 6.0, ((0, 128),)),
        "expert_in": gaussian(streams_of[9], (N_GROUP * N_EXPERT, D, 2 * FS), D ** -0.5, 0.0625, ((0, 128),)),
        "expert_out": gaussian(streams_of[10], (N_GROUP * N_EXPERT, FS, D), FFE ** -0.5, 0.15625, ((0, 128),)),
    }


EPSILON = 1e-06

def slot_columns(routes, number, capacity):
    inside = routes < number
    flattened = jnp.where(inside, routes, number).reshape(-1).astype(jnp.int32)
    labels = jnp.arange(number, dtype=jnp.int32)
    matches = (flattened[:, None] == labels[None, :]).astype(jnp.int32)
    preceding = jnp.cumsum(matches, axis=0).astype(jnp.int32) - matches
    ranked = lax.optimization_barrier(jnp.sum(preceding * matches, axis=1)).astype(jnp.int32)
    retained = (flattened < number) & (ranked < capacity)
    placed = jnp.where(retained, flattened * capacity + ranked, number * capacity)
    return placed.reshape(routes.shape).astype(jnp.int32)

def dispatch_tables(placed, gate_values, slot_total):
    labels = jnp.arange(slot_total, dtype=jnp.int32)
    matches = placed[:, :, None] == labels[None, None, :]
    chosen = jnp.any(matches, axis=1).astype(jnp.bfloat16)
    mixing = lax.optimization_barrier(jnp.sum(jnp.where(matches, gate_values[:, :, None], 0.0), axis=1)).astype(jnp.float32)
    return (chosen, mixing)

def widened(values):
    return lax.optimization_barrier(values).astype(jnp.float32)

def expert_forward(row_block, weights_in):
    joined = jnp.dot(row_block.astype(jnp.float32), weights_in.astype(jnp.float32))
    half_size = weights_in.shape[1] // 2
    gate_part = joined[:, :half_size]
    up_part = joined[:, half_size:]
    activated = (gate_part * jax.nn.sigmoid(gate_part) * up_part).astype(jnp.bfloat16)
    return (joined, activated)

def expert_backward(row_block, grad_block, joined, activated, weights_in, weights_out):
    contract_last = (((1,), (1,)), ((), ()))
    contract_first = (((0,), (0,)), ((), ()))
    weights_in_wide = weights_in.astype(jnp.float32)
    act_grad = lax.dot_general(grad_block.astype(jnp.float32), weights_out.astype(jnp.float32), contract_last)
    half_size = weights_in.shape[1] // 2
    gate_part = joined[:, :half_size]
    up_part = joined[:, half_size:]
    sigmoid_gate = jax.nn.sigmoid(gate_part)
    gate_grad = act_grad * up_part * sigmoid_gate * (1.0 + gate_part * (1.0 - sigmoid_gate))
    up_grad = act_grad * gate_part * sigmoid_gate
    joined_grad = widened(jnp.concatenate([gate_grad, up_grad], axis=1).astype(jnp.bfloat16))
    back_rows = lax.dot_general(joined_grad, weights_in_wide, contract_last).astype(jnp.bfloat16)
    grad_in = lax.dot_general(row_block.astype(jnp.float32), joined_grad, contract_first)
    grad_out = lax.dot_general(widened(activated), grad_block.astype(jnp.float32), contract_first)
    return (back_rows, grad_in, grad_out)

def normed(values, gain_vector):
    inverse_rms = lax.rsqrt(lax.optimization_barrier(jnp.mean(values * values, axis=-1, keepdims=True)) + EPSILON)
    return values * inverse_rms * gain_vector

def norm_backward(values, gain_vector, upstream):
    inverse_rms = lax.rsqrt(lax.optimization_barrier(jnp.mean(values * values, axis=-1, keepdims=True)) + EPSILON)
    scaled = gain_vector * upstream
    return inverse_rms * scaled - values * inverse_rms ** 3 * lax.optimization_barrier(jnp.mean(values * scaled, axis=-1, keepdims=True))

def forward_expert(operands):
    row_block, shards_in, shards_out = operands

    def one_shard(weights_in, weights_out):
        joined, activated = expert_forward(row_block, weights_in)
        piece = jnp.dot(widened(activated), weights_out.astype(jnp.float32)).astype(jnp.bfloat16)
        return lax.optimization_barrier(piece)
    return lax.optimization_barrier(jnp.sum(jax.vmap(one_shard)(shards_in, shards_out).astype(jnp.float32), axis=0))

def backward_expert(operands):
    row_block, grad_block, shards_in, shards_out = operands

    def one_shard(weights_in, weights_out):
        joined, activated = expert_forward(row_block, weights_in)
        back_rows, grad_in, grad_out = expert_backward(row_block, grad_block, joined, activated, weights_in, weights_out)
        return (lax.optimization_barrier(back_rows), grad_in, grad_out)
    backs, grads_in, grads_out = jax.vmap(one_shard)(shards_in, shards_out)
    return (lax.optimization_barrier(jnp.sum(backs.astype(jnp.float32), axis=0)), grads_in, grads_out)

def reference(hidden_rows, embed_rows, gain_hidden, gain_embed, main_route, main_gates, draft_route, draft_gates, draft_cotangent, expert_in, expert_out):
    blocks = N_GROUP * N_EXPERT
    features = hidden_rows.shape[1]
    inner = expert_in.shape[2]
    half_inner = expert_out.shape[1]

    def tables(routes, gate_values, number):

        def one_block(block_routes, block_gates):
            placed = slot_columns(block_routes, number, CAP)
            return dispatch_tables(placed, block_gates, number * CAP)
        return jax.vmap(one_block)(routes.reshape(blocks, TOK_DEV, TOPK), gate_values.reshape(blocks, TOK_DEV, TOPK))

    def collect(chosen, source):
        return jnp.einsum('btm,btd->bmd', chosen.astype(jnp.float32), source.astype(jnp.float32))

    def by_expert(buffer, number):
        return buffer.reshape(blocks, number, CAP, features).transpose(1, 0, 2, 3).reshape(number, blocks * CAP, features)

    def by_block(totals, number):
        return totals.reshape(number, blocks, CAP, features).transpose(1, 0, 2, 3).reshape(blocks, number * CAP, features)

    def spread(mixing, totals):
        return jnp.einsum('btm,bmd->btd', mixing, totals, precision=lax.Precision.HIGHEST)
    hidden_blocks = hidden_rows.reshape(blocks, TOK_DEV, features)
    embed_blocks = embed_rows.reshape(blocks, TOK_DEV, features).astype(jnp.float32)
    cotangent_blocks = draft_cotangent.reshape(blocks, TOK_DEV, features)
    main_in = expert_in[:MAIN_EXP * SHARDS].reshape(MAIN_EXP, SHARDS, features, inner)
    main_out = expert_out[:MAIN_EXP * SHARDS].reshape(MAIN_EXP, SHARDS, half_inner, features)
    draft_in = expert_in[MAIN_EXP * SHARDS:].reshape(EXPG, SHARDS, features, inner)
    draft_out = expert_out[MAIN_EXP * SHARDS:].reshape(EXPG, SHARDS, half_inner, features)
    main_chosen, main_mixing = tables(main_route, main_gates, MAIN_EXP)
    main_buffer = by_expert(collect(main_chosen, hidden_blocks).astype(jnp.bfloat16), MAIN_EXP)
    main_totals = lax.map(forward_expert, (main_buffer, main_in, main_out))
    settled = hidden_blocks.astype(jnp.float32) + spread(main_mixing, by_block(main_totals, MAIN_EXP))
    joined_rows = (normed(settled, gain_hidden) + normed(embed_blocks, gain_embed)).astype(jnp.bfloat16)
    draft_chosen, draft_mixing = tables(draft_route, draft_gates, EXPG)
    draft_buffer = by_expert(collect(draft_chosen, joined_rows).astype(jnp.bfloat16), EXPG)
    slot_weight = lax.optimization_barrier(jnp.sum(draft_mixing, axis=1))
    draft_signal = (slot_weight[:, :, None] * collect(draft_chosen, cotangent_blocks)).astype(jnp.bfloat16)
    draft_signal = by_expert(draft_signal, EXPG)
    draft_totals, draft_grads_in, draft_grads_out = lax.map(backward_expert, (draft_buffer, draft_signal, draft_in, draft_out))
    lifted = cotangent_blocks.astype(jnp.float32) + spread(draft_mixing, by_block(draft_totals, EXPG))
    settled_grad = norm_backward(settled, gain_hidden, lifted)
    embed_grad = norm_backward(embed_blocks, gain_embed, lifted).astype(jnp.bfloat16)
    main_signal = jnp.einsum('btm,btd->bmd', main_mixing, settled_grad, precision=lax.Precision.HIGHEST).astype(jnp.bfloat16)
    main_signal = by_expert(main_signal, MAIN_EXP)
    main_backs, main_grads_in, main_grads_out = lax.map(backward_expert, (main_buffer, main_signal, main_in, main_out))
    hidden_grad = (settled_grad + spread(main_mixing, by_block(main_backs, MAIN_EXP))).astype(jnp.bfloat16)
    in_grad = jnp.concatenate([main_grads_in.reshape(MAIN_EXP * SHARDS, features, inner), draft_grads_in.reshape(EXPG * SHARDS, features, inner)], axis=0).astype(jnp.bfloat16)
    out_grad = jnp.concatenate([main_grads_out.reshape(MAIN_EXP * SHARDS, half_inner, features), draft_grads_out.reshape(EXPG * SHARDS, half_inner, features)], axis=0).astype(jnp.bfloat16)
    return (hidden_grad.reshape(-1, features), embed_grad.reshape(-1, features), in_grad, out_grad)
```

```python
import jax
import jax.numpy as jnp
from jax import lax
from jax.sharding import Mesh, PartitionSpec as P

CAP = 2
EPSILON = 1e-06
BF16 = jnp.bfloat16
F32 = jnp.float32
AXES = ("g", "z", "y", "x")
Y_SIZE = 4
X_SIZE = 2
ALL_GROUPS = (0, 1, 2, 3)
MAIN_GROUPS = (0, 1, 2)
DRAFT_GROUPS = (3,)


def slot_columns(routes, number, capacity):
    inside = routes < number
    flattened = jnp.where(inside, routes, number).reshape(-1)
    labels = jnp.arange(number, dtype=jnp.int32)
    matches = (flattened[:, None] == labels[None, :]).astype(jnp.int32)
    preceding = jnp.cumsum(matches, axis=0) - matches
    ranked = jnp.sum(preceding * matches, axis=1)
    retained = (flattened < number) & (ranked < capacity)
    placed = jnp.where(retained, flattened * capacity + ranked, number * capacity)
    return placed.reshape(routes.shape)


def dispatch_tables(placed, gate_values, slot_total):
    labels = jnp.arange(slot_total, dtype=jnp.int32)
    matches = placed[:, :, None] == labels[None, None, :]
    chosen = jnp.any(matches, axis=1).astype(BF16)
    mixing = jnp.sum(jnp.where(matches, gate_values[:, :, None], 0.0), axis=1)
    return (chosen, mixing)


def contract(left, right, over_left, over_right):
    return lax.dot_general(
        left, right, (((over_left,), (over_right,)), ((), ())), preferred_element_type=F32
    )


def split_three(values):
    high = values.astype(BF16)
    rest = values - high.astype(F32)
    middle = rest.astype(BF16)
    low = (rest - middle.astype(F32)).astype(BF16)
    return (high, middle, low)


def weighted(mixing, rows):
    parts = jnp.concatenate(split_three(mixing), axis=1)
    return contract(parts, jnp.concatenate([rows] * 3, axis=0), 1, 0)


def mover(groups, axis, size, shift):
    pairs = []
    for group in groups:
        for place in range(size):
            pairs.append((group * size + place, group * size + (place + shift) % size))
    return lambda values: lax.ppermute(values, ("g", axis), pairs)


def movers(groups):
    return (
        mover(groups, "y", Y_SIZE, 1),
        mover(groups, "y", Y_SIZE, -1),
        mover(groups, "x", X_SIZE, 1),
    )


KEYS = [(part, dy, dx) for part in "PQ" for dy in (0, -1, 1, 2) for dx in (0, 1)]


def plane_gather(rows, groups):
    up, down, cross = movers(groups)
    half = rows.shape[0] // 2
    own_p, own_q = rows[:half], rows[half:]
    o = {("P", 0, 0): own_p, ("Q", 0, 0): own_q}
    o["P", -1, 0] = up(own_p)
    o["P", 1, 0] = down(own_p)
    o["Q", 0, 1] = cross(own_q)
    o["Q", -1, 0] = up(own_q)
    o["Q", 1, 0] = down(own_q)
    o["P", 0, 1] = cross(own_p)
    o["P", 2, 0] = up(o["P", -1, 0])
    o["Q", -1, 1] = up(o["Q", 0, 1])
    o["Q", 1, 1] = down(o["Q", 0, 1])
    o["P", -1, 1] = cross(o["P", -1, 0])
    o["P", 1, 1] = cross(o["P", 1, 0])
    o["P", 2, 1] = cross(o["P", 2, 0])
    o["Q", 2, 0] = up(o["Q", -1, 0])
    o["Q", 2, 1] = down(o["Q", 1, 1])
    return jnp.concatenate([o[key] for key in KEYS], axis=0)


def total_of(*terms):
    total = terms[0].astype(F32)
    for term in terms[1:]:
        total = total + term.astype(F32)
    return total.astype(BF16)


def plane_sum(partials, groups):
    up, down, cross = movers(groups)
    half = partials.shape[0] // len(KEYS)
    o = {key: partials[i * half : (i + 1) * half] for i, key in enumerate(KEYS)}
    far = total_of(o["P", 2, 0], cross(o["P", 2, 1]))
    q_far = up(o["Q", 2, 0])
    x_far = down(o["Q", 2, 1])
    near = {dy: total_of(o["P", dy, 0], cross(o["P", dy, 1])) for dy in (1, -1, 0)}
    q_next = total_of(o["Q", 1, 0], q_far)
    x_next = total_of(o["Q", -1, 1], x_far)
    q_own = total_of(o["Q", 0, 0], up(q_next), down(o["Q", -1, 0]))
    x_own = total_of(o["Q", 0, 1], up(o["Q", 1, 1]), down(x_next))
    q_total = total_of(q_own, cross(x_own))
    p_next = total_of(near[1], up(far))
    p_total = total_of(near[0], up(p_next), down(near[-1]))
    return jnp.concatenate([p_total, q_total], axis=0)


def exchange(rows):
    features = rows.shape[1]
    moved = lax.all_to_all(rows.reshape(-1, CAP, features), ("g", "z"), 0, 0, tiled=True)
    return moved.reshape(-1, features)


def halves(joined):
    half = joined.shape[1] // 2
    return joined[:, :half], joined[:, half:]


def activation(joined):
    gate, up = halves(joined)
    return (gate * jax.nn.sigmoid(gate) * up).astype(BF16)


def middle_grad(joined, act_grad):
    gate, up = halves(joined)
    sigmoid_gate = jax.nn.sigmoid(gate)
    gate_grad = act_grad * up * sigmoid_gate * (1.0 + gate * (1.0 - sigmoid_gate))
    up_grad = act_grad * gate * sigmoid_gate
    return jnp.concatenate([gate_grad, up_grad], axis=1).astype(BF16)


def inverse_rms(values):
    return lax.rsqrt(jnp.mean(values * values, axis=-1, keepdims=True) + EPSILON)


def norm_backward(values, inverse, scaled):
    return inverse * scaled - values * inverse**3 * jnp.mean(
        values * scaled, axis=-1, keepdims=True
    )


def on_device(
    hidden_rows,
    embed_rows,
    gain_hidden,
    gain_embed,
    main_route,
    main_gates,
    draft_route,
    draft_gates,
    draft_cotangent,
    expert_in,
    expert_out,
):
    groups = lax.axis_size("g")
    per_group = lax.axis_size("z")
    main_count = (groups - 1) * per_group
    main_slots = main_count * CAP
    draft_slots = per_group * CAP
    features = hidden_rows.shape[1]
    inward = expert_in[0]
    outward = expert_out[0]
    is_draft = lax.axis_index("g") == groups - 1

    main_placed = slot_columns(main_route, main_count, CAP)
    main_chosen, main_mixing = dispatch_tables(main_placed, main_gates, main_slots)
    draft_placed = slot_columns(draft_route, per_group, CAP)
    draft_chosen, draft_mixing = dispatch_tables(draft_placed, draft_gates, draft_slots)
    slot_weight = jnp.sum(draft_mixing, axis=0)

    main_rows = contract(main_chosen, hidden_rows, 0, 0).astype(BF16)
    draft_signal = (slot_weight[:, None] * contract(draft_chosen, draft_cotangent, 0, 0)).astype(
        BF16
    )
    first = plane_gather(
        exchange(jnp.concatenate([main_rows, draft_signal], axis=0)), ALL_GROUPS
    )
    first_joined = jnp.dot(first, inward, preferred_element_type=F32)
    first_active = activation(first_joined)
    partial_out = jnp.dot(first_active, outward, preferred_element_type=F32).astype(BF16)
    main_total = exchange(plane_sum(partial_out, MAIN_GROUPS))[:main_slots]

    picked_hidden = contract(draft_chosen, hidden_rows, 0, 0)
    picked_embed = contract(draft_chosen, embed_rows, 0, 0)
    picked_mixing = lax.dot_general(
        draft_chosen.astype(F32),
        main_mixing,
        (((0,), (0,)), ((), ())),
        precision=lax.Precision.HIGHEST,
    )
    picked_settled = picked_hidden + weighted(picked_mixing, main_total)
    taken = jnp.sum(draft_chosen.astype(F32), axis=0)[:, None]
    draft_rows = (
        taken
        * (
            picked_settled * inverse_rms(picked_settled) * gain_hidden
            + picked_embed * inverse_rms(picked_embed) * gain_embed
        )
    ).astype(BF16)
    second = plane_gather(
        exchange(jnp.concatenate([jnp.zeros((main_slots, features), BF16), draft_rows], axis=0)),
        DRAFT_GROUPS,
    )
    second_joined = jnp.dot(second, inward, preferred_element_type=F32)
    second_active = activation(second_joined)
    second_mid = middle_grad(second_joined, contract(first, outward, 1, 1))
    draft_back = contract(second_mid, inward, 1, 1).astype(BF16)
    draft_total = exchange(plane_sum(draft_back, DRAFT_GROUPS))[main_slots:]

    hidden = hidden_rows.astype(F32)
    embedded = embed_rows.astype(F32)
    settled = hidden + weighted(main_mixing, main_total)
    settled_inverse = inverse_rms(settled)
    embed_inverse = inverse_rms(embedded)
    lifted = draft_cotangent.astype(F32) + weighted(draft_mixing, draft_total)
    settled_grad = norm_backward(settled, settled_inverse, gain_hidden * lifted)
    embed_grad = norm_backward(embedded, embed_inverse, gain_embed * lifted).astype(BF16)

    main_signal = lax.dot_general(
        main_mixing,
        settled_grad,
        (((0,), (0,)), ((), ())),
        precision=lax.Precision.HIGHEST,
        preferred_element_type=F32,
    ).astype(BF16)
    third = plane_gather(
        exchange(
            jnp.concatenate([main_signal, jnp.zeros((draft_slots, features), BF16)], axis=0)
        ),
        MAIN_GROUPS,
    )
    first_mid = middle_grad(first_joined, contract(third, outward, 1, 1))
    main_back = contract(first_mid, inward, 1, 1).astype(BF16)
    main_back_total = exchange(plane_sum(main_back, MAIN_GROUPS))[:main_slots]
    hidden_grad = (settled_grad + weighted(main_mixing, main_back_total)).astype(BF16)

    final_rows = jnp.where(is_draft, second, first)
    final_signal = jnp.where(is_draft, first, third)
    final_mid = jnp.where(is_draft, second_mid, first_mid)
    final_active = jnp.where(is_draft, second_active, first_active)
    in_grad = contract(final_rows, final_mid, 0, 0).astype(BF16)[None]
    out_grad = contract(final_active, final_signal, 0, 0).astype(BF16)[None]
    return (hidden_grad, embed_grad, in_grad, out_grad)


def solution(mesh):
    fine = Mesh(mesh.devices.reshape(4, 4, Y_SIZE, X_SIZE), AXES)
    rows = P(AXES, None)
    blocks = P(AXES, None, None)
    return jax.shard_map(
        on_device,
        mesh=fine,
        in_specs=(rows, rows, P(), P(), rows, rows, rows, rows, rows, blocks, blocks),
        out_specs=(rows, rows, blocks, blocks),
        check_vma=False,
    )
```

```python
import jax
import jax.numpy as jnp
from jax import lax
from jax.experimental import pallas as pl
from jax.experimental.pallas import tpu as pltpu
from jax.sharding import Mesh, PartitionSpec as P

CAP = 2
EPSILON = 1e-06
BF16 = jnp.bfloat16
F32 = jnp.float32
AXES = ("g", "z", "y", "x")
SIZES = (4, 4, 4, 2)
LANES = 128
CHUNK = 1024
MIB = 1024 * 1024
IN_VMEM = pl.BlockSpec(memory_space=pltpu.VMEM)
ANYWHERE = pl.BlockSpec(memory_space=pl.ANY)


def mover(draft_only, dy, dx):
    _, depth, tall, wide = SIZES

    def number(g, z, y, x):
        return ((g * depth + z) * tall + y) * wide + x

    pairs = []
    for g in range(SIZES[0]):
        for z in range(depth):
            for y in range(tall):
                for x in range(wide):
                    if not draft_only or g == SIZES[0] - 1:
                        target = number(g, z, (y + dy) % tall, x ^ dx)
                    elif g < 2:
                        target = number(g ^ 1, z, y, x)
                    else:
                        target = number(g, z ^ 1, y, x)
                    pairs.append((number(g, z, y, x), target))
    return lambda values: lax.ppermute(values, AXES, pairs)


def movers(draft_only):
    return mover(draft_only, 1, 0), mover(draft_only, -1, 0), mover(draft_only, 0, 1)


def plane_gather(rows, draft_only):
    up, down, cross = movers(draft_only)
    half = rows.shape[0] // 2
    a, b = rows[:half], rows[half:]
    a_below, a_above, b_other = up(a), down(a), cross(b)
    b_below, b_above, a_other = up(b), down(b), cross(a)
    a_far = up(a_below)
    b_other_below, b_other_above = up(b_other), down(b_other)
    b_far, b_other_far = up(b_below), down(b_other_above)
    a_rest = [cross(piece) for piece in (a_below, a_above, a_far)]
    return [a, a_other, a_below, a_above, a_far, *a_rest] + [
        b, b_other, b_below, b_above, b_far, b_other_below, b_other_above, b_other_far,
    ]


def total_of(*terms):
    total = terms[0].astype(F32)
    for term in terms[1:]:
        total = total + term.astype(F32)
    return total.astype(BF16)


def plane_sum(partials, draft_only):
    up, down, cross = movers(draft_only)
    (
        a, a_other, a_below, a_above, a_far, a_other_below, a_other_above, a_other_far,
        b, b_other, b_below, b_above, b_far, b_other_below, b_other_above, b_other_far,
    ) = partials
    a_far = total_of(a_far, cross(a_other_far))
    b_above = total_of(b_above, up(b_far))
    b_other_below = total_of(b_other_below, down(b_other_far))
    a_above = total_of(a_above, cross(a_other_above))
    b_other = total_of(b_other, up(b_other_above), down(b_other_below))
    a_below = total_of(a_below, cross(a_other_below))
    a_above = total_of(a_above, up(a_far))
    b = total_of(b, up(b_above), down(b_below))
    a = total_of(a, cross(a_other))
    a = total_of(a, up(a_above), down(a_below))
    b = total_of(b, cross(b_other))
    return jnp.concatenate([a, b], axis=0)


def exchange(rows):
    features = rows.shape[1]
    moved = lax.all_to_all(rows.reshape(-1, CAP, features), ("g", "z"), 0, 0, tiled=True)
    return moved.reshape(-1, features)


def params(mebibytes=60):
    return pltpu.CompilerParams(vmem_limit_bytes=mebibytes * MIB)


def dot(left, right, over_left=1, over_right=0):
    return lax.dot_general(
        left, right, (((over_left,), (over_right,)), ((), ())), preferred_element_type=F32
    )


def split_three(values):
    high = values.astype(BF16)
    rest = values - high.astype(F32)
    middle = rest.astype(BF16)
    return (high, middle, (rest - middle.astype(F32)).astype(BF16))


def weighted(mixing, rows):
    high, middle, low = split_three(mixing)
    return dot(high, rows) + dot(middle, rows) + dot(low, rows)


def inverse_rms(values):
    return lax.rsqrt(jnp.mean(values * values, axis=-1, keepdims=True) + EPSILON)


def norm_backward(values, inverse, scaled):
    mean = jnp.mean(values * scaled, axis=-1, keepdims=True)
    return inverse * scaled - values * (inverse * inverse * inverse * mean)


def tables(main_route, main_gates, draft_route, draft_gates, hidden, embed, cotangent, counts):
    main_slots, slots = counts
    tokens, features = hidden.shape
    chunk = min(CHUNK, features)

    def body(mr, mg, dr, dg, hid, emb, cot, send, hp, cp, ep, mix, picked, weight, table, scale):
        @pl.when(pl.program_id(0) == 0)
        def _():
            slot = lax.broadcasted_iota(jnp.int32, (slots, tokens), 0)
            is_main = slot < main_slots
            label = jnp.where(is_main, slot, slot - main_slots) // CAP
            held = jnp.zeros((slots, tokens), F32)
            gates = jnp.zeros((slots, tokens), F32)
            for k in range(mr.shape[0]):
                one = slice(k, k + 1)
                hit = jnp.where(is_main, mr[one, :], dr[one, :]) == label
                held = jnp.where(hit, 1.0, held)
                gates = jnp.where(hit, jnp.where(is_main, mg[one, :], dg[one, :]), gates)
            row = lax.broadcasted_iota(jnp.int32, (tokens, tokens), 0)
            column = lax.broadcasted_iota(jnp.int32, (tokens, tokens), 1)
            before = jnp.where(row < column, 1.0, 0.0).astype(BF16)
            rank = dot(held.astype(BF16), before)
            kept = (held > 0.5) & (rank == (slot % CAP).astype(F32))
            slot_mixing = jnp.where(kept, gates, 0.0)
            chosen = jnp.where(kept, 1.0, 0.0).astype(BF16)
            spare = jnp.zeros((LANES - slots, tokens), F32)
            mixing = jnp.concatenate([slot_mixing, spare], axis=0).T
            mix[...] = mixing
            table[...] = chosen
            high, middle, low = split_three(mixing)
            picked[...] = dot(chosen, high) + dot(chosen, middle) + dot(chosen, low)
            sums = jnp.sum(slot_mixing, axis=1, keepdims=True)
            weight[...] = jnp.broadcast_to(sums, (slots, LANES))
            scale[...] = jnp.broadcast_to(sums, (slots, LANES))

        chosen = table[...]
        hidden_part = dot(chosen, hid[...])
        cotangent_part = dot(chosen, cot[...])
        slot = lax.broadcasted_iota(jnp.int32, (slots, chunk), 0)
        send[...] = jnp.where(
            slot < main_slots, hidden_part, scale[:, :1] * cotangent_part
        ).astype(BF16)
        hp[...] = hidden_part.astype(BF16)
        cp[...] = cotangent_part.astype(BF16)
        ep[...] = dot(chosen, emb[...]).astype(BF16)

    whole = pl.BlockSpec(main_route.shape, lambda i: (0, 0))
    wide = pl.BlockSpec((tokens, chunk), lambda i: (0, i))
    slim = pl.BlockSpec((slots, chunk), lambda i: (0, i))
    rows = jax.ShapeDtypeStruct((slots, features), BF16)
    small = jax.ShapeDtypeStruct((slots, LANES), F32)
    small_spec = pl.BlockSpec((slots, LANES), lambda i: (0, 0))
    return pl.pallas_call(
        body,
        grid=(features // chunk,),
        in_specs=[whole] * 4 + [wide] * 3,
        out_specs=[slim] * 4
        + [pl.BlockSpec((tokens, LANES), lambda i: (0, 0)), small_spec, small_spec],
        out_shape=[rows] * 4 + [jax.ShapeDtypeStruct((tokens, LANES), F32), small, small],
        scratch_shapes=[pltpu.VMEM((slots, tokens), BF16), pltpu.VMEM((slots, LANES), F32)],
        compiler_params=params(),
        name="slot_tables",
    )(main_route, main_gates, draft_route, draft_gates, hidden, embed, cotangent)


def lane_part(values, low, high):
    lane = lax.broadcasted_iota(jnp.int32, values.shape, 1)
    return jnp.where((lane >= low) & (lane < high), values, 0.0)


def row_part(values, low, high):
    row = lax.broadcasted_iota(jnp.int32, values.shape, 0)
    return jnp.where((row >= low) & (row < high), values, jnp.zeros_like(values))


def draft_row_kernel(hp, ep, picked, weight, main_total, gain_hidden, gain_embed, counts):
    main_slots, slots = counts

    def body(hp, ep, picked, weight, total, gain_h, gain_e, out):
        mixing = lane_part(picked[:, :slots], 0, main_slots)
        settled = hp[...].astype(F32) + weighted(mixing, row_part(total[...], 0, main_slots))
        embedded = ep[...].astype(F32)
        joined = (
            settled * inverse_rms(settled) * gain_h[...]
            + embedded * inverse_rms(embedded) * gain_e[...]
        )
        joined = jnp.where(weight[:, :1] > 0.0, joined, 0.0)
        out[...] = row_part(joined, main_slots, slots).astype(BF16)

    return pl.pallas_call(
        body,
        in_specs=[IN_VMEM] * 7,
        out_specs=IN_VMEM,
        out_shape=jax.ShapeDtypeStruct(hp.shape, BF16),
        compiler_params=params(),
        name="draft_rows",
    )(hp, ep, picked, weight, main_total, gain_hidden, gain_embed)


def main_signal_kernel(hp, cp, picked, weight, main_total, draft_total, gain_hidden, counts):
    main_slots, slots = counts

    def body(hp, cp, picked, weight, total, drafts, gain_h, out):
        mixing = picked[:, :slots]
        settled = hp[...].astype(F32) + weighted(
            lane_part(mixing, 0, main_slots), row_part(total[...], 0, main_slots)
        )
        lifted = cp[...].astype(F32) + weighted(
            lane_part(mixing, main_slots, slots), row_part(drafts[...], main_slots, slots)
        )
        grad = norm_backward(settled, inverse_rms(settled), gain_h[...] * lifted)
        out[...] = row_part(weight[:, :1] * grad, 0, main_slots).astype(BF16)

    return pl.pallas_call(
        body,
        in_specs=[IN_VMEM] * 7,
        out_specs=IN_VMEM,
        out_shape=jax.ShapeDtypeStruct(hp.shape, BF16),
        compiler_params=params(),
        name="main_signals",
    )(hp, cp, picked, weight, main_total, draft_total, gain_hidden)


def token_grad_kernel(
    hidden, embed, cotangent, mixing, main_total, draft_total, gain_hidden, gain_embed, counts
):
    main_slots, slots = counts
    tokens, features = hidden.shape
    block = 32

    def body(hid, emb, cot, mix, total, drafts, gain_h, gain_e, settled_grad, embed_grad):
        mixed = mix[:, :slots]
        settled = hid[...].astype(F32) + weighted(
            lane_part(mixed, 0, main_slots), row_part(total[...], 0, main_slots)
        )
        lifted = cot[...].astype(F32) + weighted(
            lane_part(mixed, main_slots, slots), row_part(drafts[...], main_slots, slots)
        )
        settled_grad[...] = norm_backward(settled, inverse_rms(settled), gain_h[...] * lifted)
        embedded = emb[...].astype(F32)
        embed_grad[...] = norm_backward(
            embedded, inverse_rms(embedded), gain_e[...] * lifted
        ).astype(BF16)

    wide = pl.BlockSpec((block, features), lambda i: (i, 0))
    slim = pl.BlockSpec((slots, features), lambda i: (0, 0))
    gain = pl.BlockSpec((1, features), lambda i: (0, 0))
    return pl.pallas_call(
        body,
        grid=(tokens // block,),
        in_specs=[wide] * 3
        + [pl.BlockSpec((block, LANES), lambda i: (i, 0))]
        + [slim] * 2
        + [gain] * 2,
        out_specs=[wide] * 2,
        out_shape=[
            jax.ShapeDtypeStruct(hidden.shape, F32),
            jax.ShapeDtypeStruct(hidden.shape, BF16),
        ],
        compiler_params=params(),
        cost_estimate=pl.CostEstimate(
            flops=tokens * features * 100, bytes_accessed=13 * tokens * features, transcendentals=0
        ),
        name="token_grads",
    )(hidden, embed, cotangent, mixing, main_total, draft_total, gain_hidden, gain_embed)


def hidden_grad_kernel(settled_grad, mixing, back_total, counts):
    main_slots, slots = counts
    tokens, features = settled_grad.shape
    block = 32

    def body(grad, mix, total, out):
        mixed = lane_part(mix[:, :slots], 0, main_slots)
        out[...] = (
            grad[...] + weighted(mixed, row_part(total[...], 0, main_slots))
        ).astype(BF16)

    wide = pl.BlockSpec((block, features), lambda i: (i, 0))
    return pl.pallas_call(
        body,
        grid=(tokens // block,),
        in_specs=[
            wide,
            pl.BlockSpec((block, LANES), lambda i: (i, 0)),
            pl.BlockSpec((slots, features), lambda i: (0, 0)),
        ],
        out_specs=wide,
        out_shape=jax.ShapeDtypeStruct(settled_grad.shape, BF16),
        compiler_params=params(),
        name="hidden_grads",
    )(settled_grad, mixing, back_total)


def columns(index, chunk):
    return pl.ds(index * chunk, chunk)


def row_copies(pieces, held, sems, outwards=False):
    made = []
    for i, piece in enumerate(pieces):
        size = piece.shape[0]
        inside = held.at[pl.ds(i * size, size), :]
        ends = (inside, piece) if outwards else (piece, inside)
        made.append(pltpu.make_async_copy(*ends, sems.at[i]))
    return made


def weight_copies(whole, held, sems, chunk, over_rows):
    made = []
    for c in range(sems.shape[0]):
        place = (columns(c, chunk), slice(None)) if over_rows else (slice(None), columns(c, chunk))
        made.append(pltpu.make_async_copy(whole.at[place], held.at[place], sems.at[c]))
    return made


def start_all(copies):
    for copy in copies:
        copy.start()


def wait_all(copies):
    for copy in copies:
        copy.wait()


def forward_kernel(pieces, inward, outward):
    count, size = len(pieces), pieces[0].shape[0]
    features, inner = inward.shape
    half, rows = outward.shape[0], len(pieces) * pieces[0].shape[0]
    chunk = min(CHUNK, features)
    steps = features // chunk

    def body(*refs):
        given, (w_in, w_out), refs = refs[:count], refs[count : count + 2], refs[count + 2 :]
        (joined, active), partial = refs[:2], refs[2 : 2 + count]
        x, held_in, held_out, out, x_sems, in_sems, out_sems, done_sems = refs[2 + count :]
        x_copies = row_copies(given, x, x_sems)
        in_copies = weight_copies(w_in, held_in, in_sems, chunk, True)
        out_copies = weight_copies(w_out, held_out, out_sems, chunk, False)
        start_all(x_copies + in_copies + out_copies)
        wait_all(x_copies)
        total = jnp.zeros((rows, inner), F32)
        for c in range(steps):
            in_copies[c].wait()
            total = total + dot(x[:, columns(c, chunk)], held_in[columns(c, chunk), :])
        joined[...] = total
        gate, up = total[:, :half], total[:, half:]
        act = (gate * jax.nn.sigmoid(gate) * up).astype(BF16)
        active[...] = act
        for c in range(steps):
            out_copies[c].wait()
            out[:, columns(c, chunk)] = dot(act, held_out[:, columns(c, chunk)]).astype(BF16)
        done = row_copies(partial, out, done_sems, outwards=True)
        start_all(done)
        wait_all(done)

    piece = jax.ShapeDtypeStruct((size, features), BF16)
    results = pl.pallas_call(
        body,
        in_specs=[ANYWHERE] * (count + 2),
        out_specs=[IN_VMEM] * 2 + [ANYWHERE] * count,
        out_shape=[
            jax.ShapeDtypeStruct((rows, inner), F32),
            jax.ShapeDtypeStruct((rows, half), BF16),
        ]
        + [piece] * count,
        scratch_shapes=[
            pltpu.VMEM((rows, features), BF16),
            pltpu.VMEM((features, inner), BF16),
            pltpu.VMEM((half, features), BF16),
            pltpu.VMEM((rows, features), BF16),
            pltpu.SemaphoreType.DMA((count,)),
            pltpu.SemaphoreType.DMA((steps,)),
            pltpu.SemaphoreType.DMA((steps,)),
            pltpu.SemaphoreType.DMA((count,)),
        ],
        compiler_params=params(),
        cost_estimate=pl.CostEstimate(
            flops=6 * rows * features * half, bytes_accessed=16 * MIB, transcendentals=0
        ),
        name="expert_forward",
    )(*pieces, inward, outward)
    return results[0], results[1], results[2:]


def backward_kernel(signals, inward, outward, row_pieces=None, joined_rows=None):
    count, size = len(signals), signals[0].shape[0]
    features, inner = inward.shape
    half, rows = outward.shape[0], len(signals) * signals[0].shape[0]
    chunk = min(CHUNK, features)
    steps = features // chunk
    fresh = row_pieces is not None

    def body(*refs):
        given, (w_in, w_out), refs = refs[:count], refs[count : count + 2], refs[count + 2 :]
        if fresh:
            x_given, refs = refs[:count], refs[count:]
        else:
            joined, refs = refs[0], refs[1:]
        middle, refs = refs[0], refs[1:]
        if fresh:
            active, refs = refs[0], refs[1:]
        back, refs = refs[:count], refs[count:]
        s, held_in, held_out, s_sems, in_sems, out_sems, done_sems = refs[:7]
        s_copies = row_copies(given, s, s_sems)
        in_copies = weight_copies(w_in, held_in, in_sems, chunk, True)
        out_copies = weight_copies(w_out, held_out, out_sems, chunk, False)
        start_all(s_copies + out_copies)
        if fresh:
            x, x_sems = refs[7:]
            x_copies = row_copies(x_given, x, x_sems)
            start_all(x_copies)
        start_all(in_copies)
        wait_all(s_copies)
        act_grad = jnp.zeros((rows, half), F32)
        for c in range(steps):
            out_copies[c].wait()
            part = columns(c, chunk)
            act_grad = act_grad + dot(s[:, part], held_out[:, part], 1, 1)
        if fresh:
            wait_all(x_copies)
            total = jnp.zeros((rows, inner), F32)
            for c in range(steps):
                in_copies[c].wait()
                total = total + dot(x[:, columns(c, chunk)], held_in[columns(c, chunk), :])
        else:
            total = joined[...]
        gate, up = total[:, :half], total[:, half:]
        sigmoid_gate = jax.nn.sigmoid(gate)
        gate_grad = act_grad * up * sigmoid_gate * (1.0 + gate * (1.0 - sigmoid_gate))
        up_grad = act_grad * gate * sigmoid_gate
        if fresh:
            active[...] = (gate * sigmoid_gate * up).astype(BF16)
        middle[:, :half] = gate_grad.astype(BF16)
        middle[:, half:] = up_grad.astype(BF16)
        mid = middle[...]
        for c in range(steps):
            if not fresh:
                in_copies[c].wait()
            part = columns(c, chunk)
            s[:, part] = dot(mid, held_in[part, :], 1, 1).astype(BF16)
        done = row_copies(back, s, done_sems, outwards=True)
        start_all(done)
        wait_all(done)

    piece = jax.ShapeDtypeStruct((size, features), BF16)
    extra = list(row_pieces) if fresh else [joined_rows]
    shapes = [jax.ShapeDtypeStruct((rows, inner), BF16)]
    if fresh:
        shapes.append(jax.ShapeDtypeStruct((rows, half), BF16))
    scratch = [
        pltpu.VMEM((rows, features), BF16),
        pltpu.VMEM((features, inner), BF16),
        pltpu.VMEM((half, features), BF16),
        pltpu.SemaphoreType.DMA((count,)),
        pltpu.SemaphoreType.DMA((steps,)),
        pltpu.SemaphoreType.DMA((steps,)),
        pltpu.SemaphoreType.DMA((count,)),
    ]
    if fresh:
        scratch += [pltpu.VMEM((rows, features), BF16), pltpu.SemaphoreType.DMA((count,))]
    results = pl.pallas_call(
        body,
        in_specs=[ANYWHERE] * (count + 2) + ([ANYWHERE] * count if fresh else [IN_VMEM]),
        out_specs=[IN_VMEM] * len(shapes) + [ANYWHERE] * count,
        out_shape=shapes + [piece] * count,
        scratch_shapes=scratch,
        compiler_params=params(),
        cost_estimate=pl.CostEstimate(
            flops=6 * rows * features * half, bytes_accessed=16 * MIB, transcendentals=0
        ),
        name="draft_backward" if fresh else "main_backward",
    )(*signals, inward, outward, *extra)
    return results[: len(shapes)], results[len(shapes) :]


def weight_grad_kernel(is_draft, first, second, third, middles, actives):
    count, size = len(first), first[0].shape[0]
    features, rows = first[0].shape[1], len(first) * first[0].shape[0]
    inner, half = middles[0].shape[1], actives[0].shape[1]
    chunk = min(CHUNK, features)
    steps = features // chunk

    def body(flag, *refs):
        one, two, three = refs[:count], refs[count : 2 * count], refs[2 * count : 3 * count]
        main_mid, draft_mid, main_act, draft_act, in_grad, out_grad = refs[
            3 * count : 3 * count + 6
        ]
        x, s, mid, act, in_held, out_held, x_sems, s_sems, in_sems, out_sems = refs[3 * count + 6 :]
        draft = flag[0] == 1

        @pl.when(draft)
        def _():
            start_all(row_copies(two, x, x_sems) + row_copies(one, s, s_sems))
            mid[...] = draft_mid[...]
            act[...] = draft_act[...]

        @pl.when(jnp.logical_not(draft))
        def _():
            start_all(row_copies(one, x, x_sems) + row_copies(three, s, s_sems))
            mid[...] = main_mid[...]
            act[...] = main_act[...]

        wait_all(row_copies(one, x, x_sems))
        in_copies, out_copies = [], []
        for c in range(steps):
            part = columns(c, chunk)
            in_held[part, :] = dot(x[:, part], mid[...], 0, 0).astype(BF16)
            copy = pltpu.make_async_copy(in_held.at[part, :], in_grad.at[0, part, :], in_sems.at[c])
            copy.start()
            in_copies.append(copy)
        wait_all(row_copies(one, s, s_sems))
        for c in range(steps):
            part = columns(c, chunk)
            out_held[:, part] = dot(act[...], s[:, part], 0, 0).astype(BF16)
            copy = pltpu.make_async_copy(
                out_held.at[:, part], out_grad.at[0, :, part], out_sems.at[c]
            )
            copy.start()
            out_copies.append(copy)
        wait_all(in_copies + out_copies)

    return pl.pallas_call(
        body,
        in_specs=[pl.BlockSpec(memory_space=pltpu.SMEM)]
        + [ANYWHERE] * (3 * count)
        + [IN_VMEM] * 4,
        out_specs=[ANYWHERE] * 2,
        out_shape=[
            jax.ShapeDtypeStruct((1, features, inner), BF16),
            jax.ShapeDtypeStruct((1, half, features), BF16),
        ],
        scratch_shapes=[
            pltpu.VMEM((rows, features), BF16),
            pltpu.VMEM((rows, features), BF16),
            pltpu.VMEM((rows, inner), BF16),
            pltpu.VMEM((rows, half), BF16),
            pltpu.VMEM((features, inner), BF16),
            pltpu.VMEM((half, features), BF16),
            pltpu.SemaphoreType.DMA((count,)),
            pltpu.SemaphoreType.DMA((count,)),
            pltpu.SemaphoreType.DMA((steps,)),
            pltpu.SemaphoreType.DMA((steps,)),
        ],
        compiler_params=params(),
        cost_estimate=pl.CostEstimate(
            flops=6 * rows * features * half, bytes_accessed=16 * MIB, transcendentals=0
        ),
        name="weight_grads",
    )(is_draft, *first, *second, *third, *middles, *actives)


def on_device(
    hidden_rows,
    embed_rows,
    gain_hidden,
    gain_embed,
    main_route,
    main_gates,
    draft_route,
    draft_gates,
    draft_cotangent,
    expert_in,
    expert_out,
):
    groups, per_group = SIZES[:2]
    counts = ((groups - 1) * per_group * CAP, groups * per_group * CAP)
    inward = expert_in[0]
    outward = expert_out[0]
    gain_hidden = gain_hidden[None]
    gain_embed = gain_embed[None]
    is_draft = (lax.axis_index("g") == groups - 1).astype(jnp.int32)[None]

    send, picked_hidden, picked_cotangent, picked_embed, mixing, picked_mixing, weight = tables(
        main_route.T, main_gates.T, draft_route.T, draft_gates.T, hidden_rows, embed_rows,
        draft_cotangent, counts,
    )
    first = plane_gather(exchange(send), False)
    joined, main_active, partial = forward_kernel(first, inward, outward)
    main_total = exchange(plane_sum(partial, False))

    draft_rows = draft_row_kernel(
        picked_hidden, picked_embed, picked_mixing, weight, main_total, gain_hidden, gain_embed,
        counts,
    )
    second = plane_gather(exchange(draft_rows), True)
    (draft_mid, draft_active), draft_back = backward_kernel(
        first, inward, outward, row_pieces=second
    )
    draft_total = exchange(plane_sum(draft_back, True))

    signal = main_signal_kernel(
        picked_hidden, picked_cotangent, picked_mixing, weight, main_total, draft_total,
        gain_hidden, counts,
    )
    third = plane_gather(exchange(signal), False)
    settled_grad, embed_grad = token_grad_kernel(
        hidden_rows, embed_rows, draft_cotangent, mixing, main_total, draft_total, gain_hidden,
        gain_embed, counts,
    )
    third, settled_grad = lax.optimization_barrier((third, settled_grad))
    (main_mid,), main_back = backward_kernel(third, inward, outward, joined_rows=joined)
    back_total = exchange(plane_sum(main_back, False))
    in_grad, out_grad = weight_grad_kernel(
        is_draft, first, second, third, (main_mid, draft_mid), (main_active, draft_active)
    )
    hidden_grad = hidden_grad_kernel(settled_grad, mixing, back_total, counts)
    return (hidden_grad, embed_grad, in_grad, out_grad)


def solution(mesh):
    fine = Mesh(mesh.devices.reshape(SIZES), AXES)
    rows = P(AXES, None)
    blocks = P(AXES, None, None)
    return jax.shard_map(
        on_device,
        mesh=fine,
        in_specs=(rows, rows, P(), P(), rows, rows, rows, rows, rows, blocks, blocks),
        out_specs=(rows, rows, blocks, blocks),
        check_vma=False,
    )
```

```python
import itertools

import jax
import jax.numpy as jnp
from jax import lax
from jax.experimental import pallas as pl
from jax.experimental.pallas import tpu as pltpu
from jax.sharding import Mesh, PartitionSpec as P

CAP = 2
EPSILON = 1e-06
BF16 = jnp.bfloat16
F32 = jnp.float32
AXES = ("g", "z", "y", "x")
SIZES = (4, 4, 4, 2)
LANES = 128
CHUNK = 1024
MIB = 1024 * 1024
GROUPS = 4
IN_VMEM = pl.BlockSpec(memory_space=pltpu.VMEM)
ANYWHERE = pl.BlockSpec(memory_space=pl.ANY)


def mover(draft_only, dy, dx):
    groups, depth, tall, wide = SIZES

    def number(g, z, y, x):
        return ((g * depth + z) * tall + y) * wide + x

    def target(g, z, y, x):
        if not draft_only or g == groups - 1:
            return number(g, z, (y + dy) % tall, x ^ dx)
        if dx:
            return number(g, (z + 1) % depth, y, x) if g == 1 else number(2 - g, z, y, x ^ 1)
        return number(g ^ 1, z, y, x) if g < 2 else number(g, (z + dy) % depth, y, x)

    places = itertools.product(*map(range, SIZES))
    pairs = [(number(*place), target(*place)) for place in places]
    return lambda values: lax.ppermute(values, AXES, pairs)


def movers(draft_only):
    return mover(draft_only, 1, 0), mover(draft_only, -1, 0), mover(draft_only, 0, 1)


def plane_gather(rows, draft_only):
    up, down, cross = movers(draft_only)
    half = rows.shape[0] // 2
    below, above, other = up(rows), down(rows), cross(rows)
    far = up(below)
    b_other = other[half:]
    b_other_below, b_other_above = up(b_other), down(b_other)
    a_other_below, a_other_above = cross(below[:half]), cross(above[:half])
    a_other_far, b_other_far = cross(far[:half]), down(b_other_above)
    arrays = [
        rows, below, above, other, far, b_other_below, b_other_above, b_other_far, a_other_below,
        a_other_above, a_other_far,
    ]
    a, b = 0, half
    places = [
        (4, b), (6, 0), (7, 0), (1, b), (10, 0), (8, 0), (9, 0), (3, a),
        (2, b), (4, a), (5, 0), (1, a), (2, a), (3, b), (0, a), (0, b),
    ]
    return arrays, places


def wide(values):
    return values.astype(F32)


def adder(body, name, inputs, results):
    features = inputs[0].shape[1]
    return pl.pallas_call(
        body,
        in_specs=[IN_VMEM] * len(inputs),
        out_specs=[IN_VMEM] * len(results),
        out_shape=[jax.ShapeDtypeStruct((*n, features), BF16) for n in results],
        compiler_params=params(8),
        name=name,
    )(*inputs)


def plane_sum(partials, draft_only, beside=None, beside_next=None):
    up, down, cross = movers(draft_only)
    up_first, down_first, cross_first, cross_second, up_next, down_next, last, own = partials
    half = own.shape[0] // 2
    low, high = slice(0, half), slice(half, 2 * half)

    def second(up_had, down_had, from_up, from_down, from_cross, up_out, down_out):
        up_out[low] = (wide(up_had[low]) + wide(from_up[low])).astype(BF16)
        up_out[high] = (wide(up_had[high]) + wide(from_cross[low])).astype(BF16)
        down_out[low] = (wide(down_had[low]) + wide(from_down[low])).astype(BF16)
        down_out[high] = (wide(down_had[high]) + wide(from_cross[high])).astype(BF16)

    def third(had, up_one, down_two, up_two, cross_two, a_out, b_out):
        a_out[...] = (wide(had[low]) + wide(cross_two[low]) + wide(up_two[high])).astype(BF16)
        b_out[...] = (wide(had[high]) + wide(up_one[high]) + wide(down_two[low])).astype(BF16)

    def fourth(had, down_one, down_two, up_two, cross_two, a_last, b_last, out):
        a_total = wide(had[low]) + wide(cross_two[high]) + wide(down_two[high]) + wide(a_last[...])
        b_total = wide(had[high]) + wide(down_one[high]) + wide(up_two[low]) + wide(b_last[...])
        out[: half // CAP] = paired(a_total.astype(BF16))
        out[half // CAP :] = paired(b_total.astype(BF16))

    up_one, down_one, cross_one = up(up_first), down(down_first), cross(cross_first)
    made = None
    if beside is not None:
        (up_one, down_one, cross_one), made = lax.optimization_barrier(
            ((up_one, down_one, cross_one), beside())
        )
    up_send, down_send = adder(
        second, "sums_second", [up_next, down_next, up_one, down_one, cross_one], [(2 * half,)] * 2
    )
    up_send, down_send, cross_second = lax.optimization_barrier((up_send, down_send, cross_second))
    up_two, down_two, cross_two = up(up_send), down(down_send), cross(cross_second)
    if beside_next is not None:
        (up_two, down_two, cross_two), made = lax.optimization_barrier(
            ((up_two, down_two, cross_two), beside_next(made))
        )
    a_send, b_send = adder(
        third, "sums_third", [last, up_one, down_two, up_two, cross_two], [(half,)] * 2
    )
    (total,) = adder(
        fourth,
        "sums_fourth",
        [own, down_one, down_two, up_two, cross_two, up(a_send), cross(b_send)],
        [(2 * half // CAP, CAP)],
    )
    return total, made


def exchange(rows):
    return lax.all_to_all(rows, ("g", "z"), 0, 0, tiled=True)


def flat(pairs):
    return pairs.reshape(-1, pairs.shape[-1])


def paired(rows):
    return rows.reshape(-1, CAP, rows.shape[-1])


def params(mebibytes=60):
    return pltpu.CompilerParams(vmem_limit_bytes=mebibytes * MIB)


def dot(left, right, over_left=1, over_right=0):
    return lax.dot_general(
        left, right, (((over_left,), (over_right,)), ((), ())), preferred_element_type=F32
    )


def split_three(values):
    high = values.astype(BF16)
    rest = values - high.astype(F32)
    middle = rest.astype(BF16)
    return (high, middle, (rest - middle.astype(F32)).astype(BF16))


def weighted(mixing, rows):
    parts = jnp.concatenate(split_three(mixing), axis=1)
    return dot(parts, jnp.concatenate([rows] * 3, axis=0))


def inverse_rms(values):
    return lax.rsqrt(jnp.mean(values * values, axis=-1, keepdims=True) + EPSILON)


def norm_backward(values, inverse, scaled):
    mean = jnp.mean(values * scaled, axis=-1, keepdims=True)
    return inverse * scaled - values * (inverse * inverse * inverse * mean)


def tables(main_route, main_gates, draft_route, draft_gates, hidden, cotangent, counts):
    main_slots, slots = counts
    tokens, features = hidden.shape
    chunk = features // 2

    def body(mr, mg, dr, dg, hid, cot, send, mix, picked, weight, table):
        @pl.when(pl.program_id(0) == 0)
        def _():
            slot = lax.broadcasted_iota(jnp.int32, (slots, tokens), 0)
            is_main = slot < main_slots
            label = jnp.where(is_main, slot, slot - main_slots) // CAP
            held = jnp.zeros((slots, tokens), F32)
            gates = jnp.zeros((slots, tokens), F32)
            for k in range(mr.shape[0]):
                one = slice(k, k + 1)
                hit = jnp.where(is_main, mr[one, :], dr[one, :]) == label
                held = jnp.where(hit, 1.0, held)
                gates = jnp.where(hit, jnp.where(is_main, mg[one, :], dg[one, :]), gates)
            row = lax.broadcasted_iota(jnp.int32, (tokens, tokens), 0)
            column = lax.broadcasted_iota(jnp.int32, (tokens, tokens), 1)
            before = jnp.where(row < column, 1.0, 0.0).astype(BF16)
            rank = dot(held.astype(BF16), before)
            kept = (held > 0.5) & (rank == (slot % CAP).astype(F32))
            slot_mixing = jnp.where(kept, gates, 0.0)
            chosen = jnp.where(kept, 1.0, 0.0).astype(BF16)
            spare = jnp.zeros((LANES - slots, tokens), F32)
            mixing = jnp.concatenate([slot_mixing, spare], axis=0).T
            mix[...] = mixing
            table[...] = chosen
            high, middle, low = split_three(mixing)
            picked[...] = dot(chosen, high) + dot(chosen, middle) + dot(chosen, low)
            sums = jnp.sum(slot_mixing, axis=1, keepdims=True)
            weight[...] = jnp.broadcast_to(sums, (slots, LANES))

        chosen = table[...]
        hidden_part = dot(chosen, hid[...])
        cotangent_part = dot(chosen, cot[...])
        slot = lax.broadcasted_iota(jnp.int32, (slots, chunk), 0)
        rows = jnp.where(slot < main_slots, hidden_part, weight[:, :1] * cotangent_part)
        send[...] = paired(rows.astype(BF16))

    whole = pl.BlockSpec(main_route.shape, lambda i: (0, 0))
    wide = pl.BlockSpec((tokens, chunk), lambda i: (0, i))
    slim = pl.BlockSpec((slots // CAP, CAP, chunk), lambda i: (0, 0, i))
    small = jax.ShapeDtypeStruct((slots, LANES), F32)
    small_spec = pl.BlockSpec((slots, LANES), lambda i: (0, 0))
    return pl.pallas_call(
        body,
        grid=(features // chunk,),
        in_specs=[whole] * 4 + [wide] * 2,
        out_specs=[
            slim,
            pl.BlockSpec((tokens, LANES), lambda i: (0, 0)),
            small_spec,
            small_spec,
            pl.BlockSpec((slots, tokens), lambda i: (0, 0)),
        ],
        out_shape=[
            jax.ShapeDtypeStruct((slots // CAP, CAP, features), BF16),
            jax.ShapeDtypeStruct((tokens, LANES), F32),
            small,
            small,
            jax.ShapeDtypeStruct((slots, tokens), BF16),
        ],
        compiler_params=params(),
        name="slot_tables",
    )(main_route, main_gates, draft_route, draft_gates, hidden, cotangent)


def pick_kernel(table, hidden, embed, cotangent):
    slots, tokens = table.shape
    features = hidden.shape[1]
    chunk = features // 2

    def body(table, *refs):
        chosen = table[...]
        for source, out in zip(refs[:3], refs[3:]):
            out[...] = dot(chosen, source[...]).astype(BF16)

    wide = pl.BlockSpec((tokens, chunk), lambda i: (0, i))
    slim = pl.BlockSpec((slots, chunk), lambda i: (0, i))
    return pl.pallas_call(
        body,
        grid=(features // chunk,),
        in_specs=[pl.BlockSpec((slots, tokens), lambda i: (0, 0))] + [wide] * 3,
        out_specs=[slim] * 3,
        out_shape=[jax.ShapeDtypeStruct((slots, features), BF16)] * 3,
        compiler_params=params(),
        cost_estimate=pl.CostEstimate(
            flops=6 * slots * tokens * features, bytes_accessed=8 * MIB, transcendentals=0
        ),
        name="slot_rows",
    )(table, hidden, embed, cotangent)


def lane_part(values, low, high):
    lane = lax.broadcasted_iota(jnp.int32, values.shape, 1)
    return jnp.where((lane >= low) & (lane < high), values, 0.0)


def row_part(values, low, high):
    row = lax.broadcasted_iota(jnp.int32, values.shape, 0)
    return jnp.where((row >= low) & (row < high), values, jnp.zeros_like(values))


def draft_row_kernel(hp, ep, picked, weight, main_total, gain_hidden, gain_embed, counts):
    main_slots, slots = counts

    def body(hp, ep, picked, weight, total, gain_h, gain_e, out):
        mixing = lane_part(picked[:, :slots], 0, main_slots)
        settled = hp[...].astype(F32) + weighted(mixing, flat(total[...]))
        embedded = ep[...].astype(F32)
        joined = (
            settled * inverse_rms(settled) * gain_h[...]
            + embedded * inverse_rms(embedded) * gain_e[...]
        )
        joined = jnp.where(weight[:, :1] > 0.0, joined, 0.0)
        out[...] = paired(row_part(joined, main_slots, slots).astype(BF16))

    return pl.pallas_call(
        body,
        in_specs=[IN_VMEM] * 7,
        out_specs=IN_VMEM,
        out_shape=jax.ShapeDtypeStruct(main_total.shape, BF16),
        compiler_params=params(),
        name="draft_rows",
    )(hp, ep, picked, weight, main_total, gain_hidden, gain_embed)


def main_signal_kernel(hp, cp, picked, weight, main_total, draft_total, gain_hidden, counts):
    main_slots, slots = counts

    def body(hp, cp, picked, weight, total, drafts, gain_h, out):
        mixing = picked[:, :slots]
        settled = hp[...].astype(F32) + weighted(
            lane_part(mixing, 0, main_slots), flat(total[...])
        )
        lifted = cp[...].astype(F32) + weighted(
            lane_part(mixing, main_slots, slots), flat(drafts[...])
        )
        grad = norm_backward(settled, inverse_rms(settled), gain_h[...] * lifted)
        out[...] = paired(row_part(weight[:, :1] * grad, 0, main_slots).astype(BF16))

    return pl.pallas_call(
        body,
        in_specs=[IN_VMEM] * 7,
        out_specs=IN_VMEM,
        out_shape=jax.ShapeDtypeStruct(main_total.shape, BF16),
        compiler_params=params(),
        name="main_signals",
    )(hp, cp, picked, weight, main_total, draft_total, gain_hidden)


def token_grad_kernel(
    hidden, embed, cotangent, mixing, main_total, draft_total, gain_hidden, gain_embed, counts,
    earlier=None,
):
    main_slots, slots = counts
    tokens, features = hidden.shape
    block = 16
    steps = tokens // block // 2
    first = 0 if earlier is None else steps
    held = () if earlier is None else tuple(earlier)

    def body(hid, emb, cot, mix, total, drafts, gain_h, gain_e, *refs):
        settled_grad, embed_grad = refs[-2:]
        mixed = mix[:, :slots]
        settled = hid[...].astype(F32) + weighted(
            lane_part(mixed, 0, main_slots), flat(total[...])
        )
        lifted = cot[...].astype(F32) + weighted(
            lane_part(mixed, main_slots, slots), flat(drafts[...])
        )
        settled_grad[...] = norm_backward(settled, inverse_rms(settled), gain_h[...] * lifted)
        embedded = emb[...].astype(F32)
        embed_grad[...] = norm_backward(
            embedded, inverse_rms(embedded), gain_e[...] * lifted
        ).astype(BF16)

    wide = pl.BlockSpec((block, features), lambda i: (first + i, 0))
    slim = pl.BlockSpec((slots // CAP, CAP, features), lambda i: (0, 0, 0))
    gain = pl.BlockSpec((1, features), lambda i: (0, 0))
    return pl.pallas_call(
        body,
        grid=(steps,),
        in_specs=[wide] * 3
        + [pl.BlockSpec((block, LANES), lambda i: (first + i, 0))]
        + [slim] * 2
        + [gain] * 2
        + [ANYWHERE] * len(held),
        input_output_aliases={8 + k: k for k in range(len(held))},
        out_specs=[wide] * 2,
        out_shape=[
            jax.ShapeDtypeStruct(hidden.shape, F32),
            jax.ShapeDtypeStruct(hidden.shape, BF16),
        ],
        compiler_params=params(),
        cost_estimate=pl.CostEstimate(
            flops=tokens * features * 50, bytes_accessed=6 * tokens * features, transcendentals=0
        ),
        name="token_grads",
    )(hidden, embed, cotangent, mixing, main_total, draft_total, gain_hidden, gain_embed, *held)


def hidden_grad_kernel(settled_grad, mixing, back_total, counts):
    main_slots, slots = counts
    tokens, features = settled_grad.shape
    chunk = features // 2

    def body(grad, mix, total, out):
        mixed = lane_part(mix[:, :slots], 0, main_slots)
        out[...] = (
            grad[...] + weighted(mixed, flat(total[...]))
        ).astype(BF16)

    wide = pl.BlockSpec((tokens, chunk), lambda i: (0, i))
    return pl.pallas_call(
        body,
        grid=(features // chunk,),
        in_specs=[
            wide,
            pl.BlockSpec((tokens, LANES), lambda i: (0, 0)),
            pl.BlockSpec((slots // CAP, CAP, chunk), lambda i: (0, 0, i)),
        ],
        out_specs=wide,
        out_shape=jax.ShapeDtypeStruct(settled_grad.shape, BF16),
        compiler_params=params(),
        name="hidden_grads",
    )(settled_grad, mixing, back_total)


def columns(index, chunk):
    return pl.ds(index * chunk, chunk)


def row_copies(arrays, places, held, sems):
    size = held.shape[0] // len(places)
    return [
        pltpu.make_async_copy(
            arrays[which].at[pl.ds(start, size), :], held.at[pl.ds(i * size, size), :], sems.at[i]
        )
        for i, (which, start) in enumerate(places)
    ]


def weight_copies(whole, held, sems, chunk, over_rows):
    made = []
    for c in range(sems.shape[0]):
        place = (columns(c, chunk), slice(None)) if over_rows else (slice(None), columns(c, chunk))
        made.append(pltpu.make_async_copy(whole.at[place], held.at[place], sems.at[c]))
    return made


def ahead(copies, depth=4):
    start_all(copies[:depth])

    def wait(i):
        copies[i].wait()
        start_all(copies[i + depth : i + depth + 1])

    return wait


def sent_columns(held, pairs, sems, group, chunk, steps):
    size = pairs[0].shape[0]
    first, end = group * steps // sems.shape[0], (group + 1) * steps // sems.shape[0]
    part = pl.ds(first * chunk, (end - first) * chunk)
    return [
        pltpu.make_async_copy(
            held.at[pl.ds(i * size, size), part], pair.at[:, part], sems.at[group, i]
        )
        for i, pair in enumerate(pairs)
    ]


def start_all(copies):
    for copy in copies:
        copy.start()


def wait_all(copies):
    for copy in copies:
        copy.wait()


def forward_kernel(gathered, inward, outward):
    arrays, places = gathered
    count, halves, rows = len(arrays), len(places), len(places) // 2 * arrays[0].shape[0]
    features, inner = inward.shape
    half = outward.shape[0]
    chunk = min(CHUNK, features)
    steps = features // chunk
    groups = min(GROUPS, steps)

    def body(*refs):
        given, (w_in, w_out), refs = refs[:count], refs[count : count + 2], refs[count + 2 :]
        (joined, active), partial = refs[:2], refs[2 : 2 + halves // 2]
        x, held_in, held_out, out, x_sems, in_sems, out_sems, done_sems = refs[2 + halves // 2 :]
        x_copies = row_copies(given, places, x, x_sems)
        start_all(x_copies)
        wait_weight = ahead(
            weight_copies(w_in, held_in, in_sems, chunk, True)
            + weight_copies(w_out, held_out, out_sems, chunk, False)
        )
        wait_all(x_copies)
        total = jnp.zeros((rows, inner), F32)
        for c in range(steps):
            wait_weight(c)
            total = total + dot(x[:, columns(c, chunk)], held_in[columns(c, chunk), :])
        joined[...] = total
        gate, up = total[:, :half], total[:, half:]
        act = (gate * jax.nn.sigmoid(gate) * up).astype(BF16)
        active[...] = act
        done = []
        for c in range(steps):
            wait_weight(steps + c)
            out[:, columns(c, chunk)] = dot(act, held_out[:, columns(c, chunk)]).astype(BF16)
            if (c + 1) * groups // steps > c * groups // steps:
                group = (c + 1) * groups // steps - 1
                copies = sent_columns(out, partial, done_sems, group, chunk, steps)
                start_all(copies)
                done += copies
        wait_all(done)

    pair = jax.ShapeDtypeStruct((2 * rows // halves, features), BF16)
    results = pl.pallas_call(
        body,
        in_specs=[ANYWHERE] * (count + 2),
        out_specs=[IN_VMEM] * 2 + [ANYWHERE] * (halves // 2),
        out_shape=[
            jax.ShapeDtypeStruct((rows, inner), F32),
            jax.ShapeDtypeStruct((rows, half), BF16),
        ]
        + [pair] * (halves // 2),
        scratch_shapes=[
            pltpu.VMEM((rows, features), BF16),
            pltpu.VMEM((features, inner), BF16),
            pltpu.VMEM((half, features), BF16),
            pltpu.VMEM((rows, features), BF16),
            pltpu.SemaphoreType.DMA((halves,)),
            pltpu.SemaphoreType.DMA((steps,)),
            pltpu.SemaphoreType.DMA((steps,)),
            pltpu.SemaphoreType.DMA((groups, halves // 2)),
        ],
        compiler_params=params(),
        cost_estimate=pl.CostEstimate(
            flops=6 * rows * features * half, bytes_accessed=16 * MIB, transcendentals=0
        ),
        name="expert_forward",
    )(*arrays, inward, outward)
    return results[0], results[1], results[2:]


def backward_kernel(signals, inward, outward, row_pieces=None, joined_rows=None):
    arrays, places = signals
    count, halves, rows = len(arrays), len(places), len(places) // 2 * arrays[0].shape[0]
    features, inner = inward.shape
    half = outward.shape[0]
    chunk = min(CHUNK, features)
    steps = features // chunk
    groups = min(GROUPS, steps)
    fresh = row_pieces is not None

    def body(*refs):
        given, (w_in, w_out), refs = refs[:count], refs[count : count + 2], refs[count + 2 :]
        if fresh:
            x_given, refs = refs[:count], refs[count:]
        else:
            joined, refs = refs[0], refs[1:]
        middle, refs = refs[0], refs[1:]
        if fresh:
            active, refs = refs[0], refs[1:]
        back, refs = refs[: halves // 2], refs[halves // 2 :]
        s, held_in, held_out, s_sems, in_sems, out_sems, done_sems = refs[:7]
        s_copies = row_copies(given, places, s, s_sems)
        in_copies = weight_copies(w_in, held_in, in_sems, chunk, True)
        out_copies = weight_copies(w_out, held_out, out_sems, chunk, False)
        start_all(s_copies)
        if fresh:
            x, x_sems = refs[7:]
            x_copies = row_copies(x_given, places, x, x_sems)
            start_all(x_copies)
        wait_weight = ahead(out_copies + in_copies)
        wait_all(s_copies)
        act_grad = jnp.zeros((rows, half), F32)
        for c in range(steps):
            wait_weight(c)
            part = columns(c, chunk)
            act_grad = act_grad + dot(s[:, part], held_out[:, part], 1, 1)
        if fresh:
            wait_all(x_copies)
            total = jnp.zeros((rows, inner), F32)
            for c in range(steps):
                wait_weight(steps + c)
                total = total + dot(x[:, columns(c, chunk)], held_in[columns(c, chunk), :])
        else:
            total = joined[...]
        gate, up = total[:, :half], total[:, half:]
        sigmoid_gate = jax.nn.sigmoid(gate)
        gate_grad = act_grad * up * sigmoid_gate * (1.0 + gate * (1.0 - sigmoid_gate))
        up_grad = act_grad * gate * sigmoid_gate
        if fresh:
            active[...] = (gate * sigmoid_gate * up).astype(BF16)
        middle[:, :half] = gate_grad.astype(BF16)
        middle[:, half:] = up_grad.astype(BF16)
        mid = middle[...]
        done = []
        for c in range(steps):
            if not fresh:
                wait_weight(steps + c)
            part = columns(c, chunk)
            s[:, part] = dot(mid, held_in[part, :], 1, 1).astype(BF16)
            if (c + 1) * groups // steps > c * groups // steps:
                group = (c + 1) * groups // steps - 1
                copies = sent_columns(s, back, done_sems, group, chunk, steps)
                start_all(copies)
                done += copies
        wait_all(done)

    pair = jax.ShapeDtypeStruct((2 * rows // halves, features), BF16)
    extra = row_pieces[0] if fresh else [joined_rows]
    shapes = [jax.ShapeDtypeStruct((rows, inner), BF16)]
    if fresh:
        shapes.append(jax.ShapeDtypeStruct((rows, half), BF16))
    scratch = [
        pltpu.VMEM((rows, features), BF16),
        pltpu.VMEM((features, inner), BF16),
        pltpu.VMEM((half, features), BF16),
        pltpu.SemaphoreType.DMA((halves,)),
        pltpu.SemaphoreType.DMA((steps,)),
        pltpu.SemaphoreType.DMA((steps,)),
        pltpu.SemaphoreType.DMA((groups, halves // 2)),
    ]
    if fresh:
        scratch += [pltpu.VMEM((rows, features), BF16), pltpu.SemaphoreType.DMA((halves,))]
    results = pl.pallas_call(
        body,
        in_specs=[ANYWHERE] * (count + 2) + ([ANYWHERE] * count if fresh else [IN_VMEM]),
        out_specs=[IN_VMEM] * len(shapes) + [ANYWHERE] * (halves // 2),
        out_shape=shapes + [pair] * (halves // 2),
        scratch_shapes=scratch,
        compiler_params=params(),
        cost_estimate=pl.CostEstimate(
            flops=6 * rows * features * half, bytes_accessed=16 * MIB, transcendentals=0
        ),
        name="draft_backward" if fresh else "main_backward",
    )(*arrays, inward, outward, *extra)
    return results[: len(shapes)], results[len(shapes) :]


def weight_grad_kernel(is_draft, first, second, third, middles, actives):
    (first, places), second, third = first, second[0], third[0]
    count, halves, rows = len(first), len(places), len(places) // 2 * first[0].shape[0]
    features = first[0].shape[1]
    inner, half = middles[0].shape[1], actives[0].shape[1]
    chunk = min(CHUNK, features)
    steps = features // chunk

    def body(flag, *refs):
        one, two, three = refs[:count], refs[count : 2 * count], refs[2 * count : 3 * count]
        main_mid, draft_mid, main_act, draft_act, in_grad, out_grad = refs[
            3 * count : 3 * count + 6
        ]
        x, s, mid, act, in_held, out_held, x_sems, s_sems, in_sems, out_sems = refs[3 * count + 6 :]
        draft = flag[0] == 1

        @pl.when(draft)
        def _():
            start_all(row_copies(two, places, x, x_sems) + row_copies(one, places, s, s_sems))
            mid[...] = draft_mid[...]
            act[...] = draft_act[...]

        @pl.when(jnp.logical_not(draft))
        def _():
            start_all(row_copies(one, places, x, x_sems) + row_copies(three, places, s, s_sems))
            mid[...] = main_mid[...]
            act[...] = main_act[...]

        wait_all(row_copies(one, places, x, x_sems))
        in_copies, out_copies = [], []
        for c in range(steps):
            part = columns(c, chunk)
            in_held[part, :] = dot(x[:, part], mid[...], 0, 0).astype(BF16)
            copy = pltpu.make_async_copy(in_held.at[part, :], in_grad.at[0, part, :], in_sems.at[c])
            copy.start()
            in_copies.append(copy)
        wait_all(row_copies(one, places, s, s_sems))
        for c in range(steps):
            part = columns(c, chunk)
            out_held[:, part] = dot(act[...], s[:, part], 0, 0).astype(BF16)
            copy = pltpu.make_async_copy(
                out_held.at[:, part], out_grad.at[0, :, part], out_sems.at[c]
            )
            copy.start()
            out_copies.append(copy)
        wait_all(in_copies + out_copies)

    return pl.pallas_call(
        body,
        in_specs=[pl.BlockSpec(memory_space=pltpu.SMEM)]
        + [ANYWHERE] * (3 * count)
        + [IN_VMEM] * 4,
        out_specs=[ANYWHERE] * 2,
        out_shape=[
            jax.ShapeDtypeStruct((1, features, inner), BF16),
            jax.ShapeDtypeStruct((1, half, features), BF16),
        ],
        scratch_shapes=[
            pltpu.VMEM((rows, features), BF16),
            pltpu.VMEM((rows, features), BF16),
            pltpu.VMEM((rows, inner), BF16),
            pltpu.VMEM((rows, half), BF16),
            pltpu.VMEM((features, inner), BF16),
            pltpu.VMEM((half, features), BF16),
            pltpu.SemaphoreType.DMA((halves,)),
            pltpu.SemaphoreType.DMA((halves,)),
            pltpu.SemaphoreType.DMA((steps,)),
            pltpu.SemaphoreType.DMA((steps,)),
        ],
        compiler_params=params(),
        cost_estimate=pl.CostEstimate(
            flops=6 * rows * features * half, bytes_accessed=16 * MIB, transcendentals=0
        ),
        name="weight_grads",
    )(is_draft, *first, *second, *third, *middles, *actives)


def on_device(
    hidden_rows,
    embed_rows,
    gain_hidden,
    gain_embed,
    main_route,
    main_gates,
    draft_route,
    draft_gates,
    draft_cotangent,
    expert_in,
    expert_out,
):
    groups, per_group = SIZES[:2]
    counts = ((groups - 1) * per_group * CAP, groups * per_group * CAP)
    inward = expert_in[0]
    outward = expert_out[0]
    gain_hidden = gain_hidden[None]
    gain_embed = gain_embed[None]
    is_draft = (lax.axis_index("g") == groups - 1).astype(jnp.int32)[None]

    send, mixing, picked_mixing, weight, table = tables(
        main_route.T, main_gates.T, draft_route.T, draft_gates.T, hidden_rows, draft_cotangent,
        counts,
    )
    first = plane_gather(flat(exchange(send)), False)
    joined, main_active, partial = forward_kernel(first, inward, outward)
    main_sum, (picked_hidden, picked_embed, picked_cotangent) = plane_sum(
        partial, False, lambda: pick_kernel(table, hidden_rows, embed_rows, draft_cotangent)
    )
    main_total = exchange(main_sum)

    draft_rows = draft_row_kernel(
        picked_hidden, picked_embed, picked_mixing, weight, main_total, gain_hidden, gain_embed,
        counts,
    )
    second = plane_gather(flat(exchange(draft_rows)), True)
    (draft_mid, draft_active), draft_back = backward_kernel(
        first, inward, outward, row_pieces=second
    )
    draft_total = exchange(plane_sum(draft_back, True)[0])

    signal = main_signal_kernel(
        picked_hidden, picked_cotangent, picked_mixing, weight, main_total, draft_total,
        gain_hidden, counts,
    )
    third = plane_gather(flat(exchange(signal)), False)
    (main_mid,), main_back = backward_kernel(third, inward, outward, joined_rows=joined)
    token_args = (
        hidden_rows, embed_rows, draft_cotangent, mixing, main_total, draft_total, gain_hidden,
        gain_embed, counts,
    )
    back_sum, (settled_grad, embed_grad) = plane_sum(
        main_back,
        False,
        lambda: token_grad_kernel(*token_args),
        lambda early: token_grad_kernel(*token_args, earlier=early),
    )
    back_total = exchange(back_sum)
    in_grad, out_grad = weight_grad_kernel(
        is_draft, first, second, third, (main_mid, draft_mid), (main_active, draft_active)
    )
    hidden_grad = hidden_grad_kernel(settled_grad, mixing, back_total, counts)
    return (hidden_grad, embed_grad, in_grad, out_grad)


def solution(mesh):
    fine = Mesh(mesh.devices.reshape(SIZES), AXES)
    rows = P(AXES, None)
    blocks = P(AXES, None, None)
    return jax.shard_map(
        on_device,
        mesh=fine,
        in_specs=(rows, rows, P(), P(), rows, rows, rows, rows, rows, blocks, blocks),
        out_specs=(rows, rows, blocks, blocks),
        check_vma=False,
    )
```

```python
import itertools

import jax
import jax.numpy as jnp
from jax import lax
from jax.experimental import pallas as pl
from jax.experimental.pallas import tpu as pltpu
from jax.sharding import Mesh, PartitionSpec as P

CAP = 2
EPSILON = 1e-06
BF16 = jnp.bfloat16
F32 = jnp.float32
AXES = ("g", "z", "y", "x")
SIZES = (4, 4, 4, 2)
LANES = 128
CHUNK = 1792
MIB = 1024 * 1024
GROUPS = 4
IN_VMEM = pl.BlockSpec(memory_space=pltpu.VMEM)
ANYWHERE = pl.BlockSpec(memory_space=pl.ANY)


def mover(draft_only, dy, dx):
    groups, depth, tall, wide = SIZES

    def number(g, z, y, x):
        return ((g * depth + z) * tall + y) * wide + x

    def target(g, z, y, x):
        if not draft_only or g == groups - 1:
            return number(g, z, (y + dy) % tall, x ^ dx)
        if dx:
            return number(g, (z + 1) % depth, y, x) if g == 1 else number(2 - g, z, y, x ^ 1)
        return number(g ^ 1, z, y, x) if g < 2 else number(g, (z + dy) % depth, y, x)

    places = itertools.product(*map(range, SIZES))
    pairs = [(number(*place), target(*place)) for place in places]
    return lambda values: lax.ppermute(values, AXES, pairs)


def movers(draft_only):
    return mover(draft_only, 1, 0), mover(draft_only, -1, 0), mover(draft_only, 0, 1)


def plane_gather(rows, draft_only, beside=None):
    up, down, cross = movers(draft_only)
    half = rows.shape[0] // 2
    below, above, other = up(rows), down(rows), cross(rows)
    made = None
    if beside is not None:
        (below, above, other), made = lax.optimization_barrier(((below, above, other), beside()))
    far = up(below)
    b_other = other[half:]
    b_other_below, b_other_above = up(b_other), down(b_other)
    a_other_below, a_other_above = cross(below[:half]), cross(above[:half])
    a_other_far, b_other_far = cross(far[:half]), down(b_other_above)
    arrays = [
        rows, below, above, other, far, b_other_below, b_other_above, b_other_far, a_other_below,
        a_other_above, a_other_far,
    ]
    return arrays, made


PLACES = ((0, 0), (-1, 0), (1, 0), (0, 1), (2, 0), (-1, 1), (1, 1), (2, 1))
PLAIN = (
    (0, 0), (0, 1), (1, 0), (1, 1), (2, 0), (2, 1), (3, 0), (3, 1),
    (4, 0), (4, 1), (8, 0), (5, 0), (9, 0), (6, 0), (10, 0), (7, 0),
)
PAIRS = (
    (4, 1), (6, 0), (7, 0), (1, 1), (10, 0), (8, 0), (9, 0), (3, 0),
    (2, 1), (4, 0), (5, 0), (1, 0), (2, 0), (3, 1), (0, 0), (0, 1),
)


def plane_sum_direct(partials, draft_only):
    sent = [
        mover(draft_only, dy, dx)(partial)
        for (dy, dx), partial in reversed(list(zip(PLACES, partials))[1:])
    ]

    def body(*refs):
        total = wide(refs[0][...])
        for ref in refs[1:-1]:
            total = total + wide(ref[...])
        refs[-1][...] = paired(total.astype(BF16))

    size = partials[0].shape[0]
    return adder(body, "sums_direct", [partials[0], *sent], [(size // CAP, CAP)])[0]


def wide(values):
    return values.astype(F32)


def adder(body, name, inputs, results):
    features = inputs[0].shape[1]
    return pl.pallas_call(
        body,
        in_specs=[IN_VMEM] * len(inputs),
        out_specs=[IN_VMEM] * len(results),
        out_shape=[jax.ShapeDtypeStruct((*n, features), BF16) for n in results],
        compiler_params=params(8),
        name=name,
    )(*inputs)


def plane_sum(partials, draft_only, beside=None, beside_next=None):
    up, down, cross = movers(draft_only)
    up_first, down_first, cross_first, cross_second, up_next, down_next, last, own = partials
    half = own.shape[0] // 2
    low, high = slice(0, half), slice(half, 2 * half)

    def second(up_had, down_had, from_up, from_down, from_cross, up_out, down_out):
        up_out[low] = (wide(up_had[low]) + wide(from_up[low])).astype(BF16)
        up_out[high] = (wide(up_had[high]) + wide(from_cross[low])).astype(BF16)
        down_out[low] = (wide(down_had[low]) + wide(from_down[low])).astype(BF16)
        down_out[high] = (wide(down_had[high]) + wide(from_cross[high])).astype(BF16)

    def third(had, up_one, down_two, up_two, cross_two, a_out, b_out):
        a_out[...] = (wide(had[low]) + wide(cross_two[low]) + wide(up_two[high])).astype(BF16)
        b_out[...] = (wide(had[high]) + wide(up_one[high]) + wide(down_two[low])).astype(BF16)

    def fourth(had, down_one, down_two, up_two, cross_two, a_last, b_last, out):
        a_total = wide(had[low]) + wide(cross_two[high]) + wide(down_two[high]) + wide(a_last[...])
        b_total = wide(had[high]) + wide(down_one[high]) + wide(up_two[low]) + wide(b_last[...])
        out[: half // CAP] = paired(a_total.astype(BF16))
        out[half // CAP :] = paired(b_total.astype(BF16))

    up_one, down_one, cross_one = up(up_first), down(down_first), cross(cross_first)
    made = None
    if beside is not None:
        (up_one, down_one, cross_one), made = lax.optimization_barrier(
            ((up_one, down_one, cross_one), beside())
        )
    up_send, down_send = adder(
        second, "sums_second", [up_next, down_next, up_one, down_one, cross_one], [(2 * half,)] * 2
    )
    up_send, down_send, cross_second = lax.optimization_barrier((up_send, down_send, cross_second))
    up_two, down_two, cross_two = up(up_send), down(down_send), cross(cross_second)
    if beside_next is not None:
        (up_two, down_two, cross_two), made = lax.optimization_barrier(
            ((up_two, down_two, cross_two), beside_next(made))
        )
    a_send, b_send = adder(
        third, "sums_third", [last, up_one, down_two, up_two, cross_two], [(half,)] * 2
    )
    (total,) = adder(
        fourth,
        "sums_fourth",
        [own, down_one, down_two, up_two, cross_two, up(a_send), cross(b_send)],
        [(2 * half // CAP, CAP)],
    )
    return total, made


def exchange(rows):
    return lax.all_to_all(rows, ("g", "z"), 0, 0, tiled=True)


def flat(pairs):
    return pairs.reshape(-1, pairs.shape[-1])


def paired(rows):
    return rows.reshape(-1, CAP, rows.shape[-1])


def params(mebibytes=60):
    return pltpu.CompilerParams(vmem_limit_bytes=mebibytes * MIB)


def dot(left, right, over_left=1, over_right=0):
    return lax.dot_general(
        left, right, (((over_left,), (over_right,)), ((), ())), preferred_element_type=F32
    )


def split_three(values):
    high = values.astype(BF16)
    rest = values - high.astype(F32)
    middle = rest.astype(BF16)
    return (high, middle, (rest - middle.astype(F32)).astype(BF16))


def weighted(mixing, rows):
    parts = jnp.concatenate(split_three(mixing), axis=1)
    return dot(parts, jnp.concatenate([rows] * 3, axis=0))


def inverse_rms(values):
    return lax.rsqrt(jnp.mean(values * values, axis=-1, keepdims=True) + EPSILON)


def norm_backward(values, inverse, scaled):
    mean = jnp.mean(values * scaled, axis=-1, keepdims=True)
    return inverse * scaled - values * (inverse * inverse * inverse * mean)


def tables(main_route, main_gates, draft_route, draft_gates, hidden, cotangent, counts):
    main_slots, slots = counts
    tokens, features = hidden.shape
    chunk = features // 2

    def body(mr, mg, dr, dg, hid, cot, send, mix, picked, weight, table):
        @pl.when(pl.program_id(0) == 0)
        def _():
            slot = lax.broadcasted_iota(jnp.int32, (slots, tokens), 0)
            is_main = slot < main_slots
            label = jnp.where(is_main, slot, slot - main_slots) // CAP
            held = jnp.zeros((slots, tokens), F32)
            gates = jnp.zeros((slots, tokens), F32)
            for k in range(mr.shape[0]):
                one = slice(k, k + 1)
                hit = jnp.where(is_main, mr[one, :], dr[one, :]) == label
                held = jnp.where(hit, 1.0, held)
                gates = jnp.where(hit, jnp.where(is_main, mg[one, :], dg[one, :]), gates)
            row = lax.broadcasted_iota(jnp.int32, (tokens, tokens), 0)
            column = lax.broadcasted_iota(jnp.int32, (tokens, tokens), 1)
            before = jnp.where(row < column, 1.0, 0.0).astype(BF16)
            rank = dot(held.astype(BF16), before)
            kept = (held > 0.5) & (rank == (slot % CAP).astype(F32))
            slot_mixing = jnp.where(kept, gates, 0.0)
            chosen = jnp.where(kept, 1.0, 0.0).astype(BF16)
            spare = jnp.zeros((LANES - slots, tokens), F32)
            mixing = jnp.concatenate([slot_mixing, spare], axis=0).T
            mix[...] = mixing
            table[...] = chosen
            high, middle, low = split_three(mixing)
            picked[...] = dot(chosen, high) + dot(chosen, middle) + dot(chosen, low)
            sums = jnp.sum(slot_mixing, axis=1, keepdims=True)
            weight[...] = jnp.broadcast_to(sums, (slots, LANES))

        chosen = table[...]
        hidden_part = dot(chosen, hid[...])
        cotangent_part = dot(chosen, cot[...])
        slot = lax.broadcasted_iota(jnp.int32, (slots, chunk), 0)
        rows = jnp.where(slot < main_slots, hidden_part, weight[:, :1] * cotangent_part)
        send[...] = paired(rows.astype(BF16))

    whole = pl.BlockSpec(main_route.shape, lambda i: (0, 0))
    wide = pl.BlockSpec((tokens, chunk), lambda i: (0, i))
    slim = pl.BlockSpec((slots // CAP, CAP, chunk), lambda i: (0, 0, i))
    small = jax.ShapeDtypeStruct((slots, LANES), F32)
    small_spec = pl.BlockSpec((slots, LANES), lambda i: (0, 0))
    return pl.pallas_call(
        body,
        grid=(features // chunk,),
        in_specs=[whole] * 4 + [wide] * 2,
        out_specs=[
            slim,
            pl.BlockSpec((tokens, LANES), lambda i: (0, 0)),
            small_spec,
            small_spec,
            pl.BlockSpec((slots, tokens), lambda i: (0, 0)),
        ],
        out_shape=[
            jax.ShapeDtypeStruct((slots // CAP, CAP, features), BF16),
            jax.ShapeDtypeStruct((tokens, LANES), F32),
            small,
            small,
            jax.ShapeDtypeStruct((slots, tokens), BF16),
        ],
        compiler_params=params(),
        name="slot_tables",
    )(main_route, main_gates, draft_route, draft_gates, hidden, cotangent)


def pick_kernel(table, hidden, embed, cotangent):
    slots, tokens = table.shape
    features = hidden.shape[1]
    chunk = features // 2

    def body(table, *refs):
        chosen = table[...]
        for source, out in zip(refs[:3], refs[3:]):
            out[...] = dot(chosen, source[...]).astype(BF16)

    wide = pl.BlockSpec((tokens, chunk), lambda i: (0, i))
    slim = pl.BlockSpec((slots, chunk), lambda i: (0, i))
    return pl.pallas_call(
        body,
        grid=(features // chunk,),
        in_specs=[pl.BlockSpec((slots, tokens), lambda i: (0, 0))] + [wide] * 3,
        out_specs=[slim] * 3,
        out_shape=[jax.ShapeDtypeStruct((slots, features), BF16)] * 3,
        compiler_params=params(),
        cost_estimate=pl.CostEstimate(
            flops=6 * slots * tokens * features, bytes_accessed=8 * MIB, transcendentals=0
        ),
        name="slot_rows",
    )(table, hidden, embed, cotangent)


def lane_part(values, low, high):
    lane = lax.broadcasted_iota(jnp.int32, values.shape, 1)
    return jnp.where((lane >= low) & (lane < high), values, 0.0)


def row_part(values, low, high):
    row = lax.broadcasted_iota(jnp.int32, values.shape, 0)
    return jnp.where((row >= low) & (row < high), values, jnp.zeros_like(values))


def draft_row_kernel(hp, ep, picked, weight, main_total, gain_hidden, gain_embed, counts):
    main_slots, slots = counts

    def body(hp, ep, picked, weight, total, gain_h, gain_e, out):
        mixing = lane_part(picked[:, :slots], 0, main_slots)
        settled = hp[...].astype(F32) + weighted(mixing, flat(total[...]))
        embedded = ep[...].astype(F32)
        joined = (
            settled * inverse_rms(settled) * gain_h[...]
            + embedded * inverse_rms(embedded) * gain_e[...]
        )
        joined = jnp.where(weight[:, :1] > 0.0, joined, 0.0)
        out[...] = paired(row_part(joined, main_slots, slots).astype(BF16))

    return pl.pallas_call(
        body,
        in_specs=[IN_VMEM] * 7,
        out_specs=IN_VMEM,
        out_shape=jax.ShapeDtypeStruct(main_total.shape, BF16),
        compiler_params=params(),
        name="draft_rows",
    )(hp, ep, picked, weight, main_total, gain_hidden, gain_embed)


def main_signal_kernel(hp, cp, picked, weight, main_total, draft_total, gain_hidden, counts):
    main_slots, slots = counts

    def body(hp, cp, picked, weight, total, drafts, gain_h, out):
        mixing = picked[:, :slots]
        settled = hp[...].astype(F32) + weighted(
            lane_part(mixing, 0, main_slots), flat(total[...])
        )
        lifted = cp[...].astype(F32) + weighted(
            lane_part(mixing, main_slots, slots), flat(drafts[...])
        )
        grad = norm_backward(settled, inverse_rms(settled), gain_h[...] * lifted)
        out[...] = paired(row_part(weight[:, :1] * grad, 0, main_slots).astype(BF16))

    return pl.pallas_call(
        body,
        in_specs=[IN_VMEM] * 7,
        out_specs=IN_VMEM,
        out_shape=jax.ShapeDtypeStruct(main_total.shape, BF16),
        compiler_params=params(),
        name="main_signals",
    )(hp, cp, picked, weight, main_total, draft_total, gain_hidden)


def token_grad_kernel(
    hidden, embed, cotangent, mixing, main_total, draft_total, gain_hidden, gain_embed, counts,
    earlier=None,
):
    main_slots, slots = counts
    tokens, features = hidden.shape
    block = 16
    steps = tokens // block // 2
    first = 0 if earlier is None else steps
    held = () if earlier is None else tuple(earlier)

    def body(hid, emb, cot, mix, total, drafts, gain_h, gain_e, *refs):
        settled_grad, embed_grad = refs[-2:]
        mixed = mix[:, :slots]
        settled = hid[...].astype(F32) + weighted(
            lane_part(mixed, 0, main_slots), flat(total[...])
        )
        lifted = cot[...].astype(F32) + weighted(
            lane_part(mixed, main_slots, slots), flat(drafts[...])
        )
        settled_grad[...] = norm_backward(settled, inverse_rms(settled), gain_h[...] * lifted)
        embedded = emb[...].astype(F32)
        embed_grad[...] = norm_backward(
            embedded, inverse_rms(embedded), gain_e[...] * lifted
        ).astype(BF16)

    wide = pl.BlockSpec((block, features), lambda i: (first + i, 0))
    slim = pl.BlockSpec((slots // CAP, CAP, features), lambda i: (0, 0, 0))
    gain = pl.BlockSpec((1, features), lambda i: (0, 0))
    return pl.pallas_call(
        body,
        grid=(steps,),
        in_specs=[wide] * 3
        + [pl.BlockSpec((block, LANES), lambda i: (first + i, 0))]
        + [slim] * 2
        + [gain] * 2
        + [ANYWHERE] * len(held),
        input_output_aliases={8 + k: k for k in range(len(held))},
        out_specs=[wide] * 2,
        out_shape=[
            jax.ShapeDtypeStruct(hidden.shape, F32),
            jax.ShapeDtypeStruct(hidden.shape, BF16),
        ],
        compiler_params=params(),
        cost_estimate=pl.CostEstimate(
            flops=tokens * features * 50, bytes_accessed=6 * tokens * features, transcendentals=0
        ),
        name="token_grads",
    )(hidden, embed, cotangent, mixing, main_total, draft_total, gain_hidden, gain_embed, *held)


def hidden_grad_kernel(settled_grad, mixing, back_total, counts):
    main_slots, slots = counts
    tokens, features = settled_grad.shape
    chunk = features // 2

    def body(grad, mix, total, out):
        mixed = lane_part(mix[:, :slots], 0, main_slots)
        out[...] = (
            grad[...] + weighted(mixed, flat(total[...]))
        ).astype(BF16)

    wide = pl.BlockSpec((tokens, chunk), lambda i: (0, i))
    return pl.pallas_call(
        body,
        grid=(features // chunk,),
        in_specs=[
            wide,
            pl.BlockSpec((tokens, LANES), lambda i: (0, 0)),
            pl.BlockSpec((slots // CAP, CAP, chunk), lambda i: (0, 0, i)),
        ],
        out_specs=wide,
        out_shape=jax.ShapeDtypeStruct(settled_grad.shape, BF16),
        compiler_params=params(),
        name="hidden_grads",
    )(settled_grad, mixing, back_total)


def columns(index, chunk):
    return pl.ds(index * chunk, chunk)


def row_copies(arrays, places, held, sems):
    size = held.shape[0] // len(places)
    return [
        pltpu.make_async_copy(
            arrays[which].at[pl.ds(half * size, size), :],
            held.at[pl.ds(i * size, size), :],
            sems.at[i],
        )
        for i, (which, half) in enumerate(places)
    ]


def weight_copies(whole, held, sems, chunk, over_rows):
    made = []
    for c in range(sems.shape[0]):
        place = (columns(c, chunk), slice(None)) if over_rows else (slice(None), columns(c, chunk))
        made.append(pltpu.make_async_copy(whole.at[place], held.at[place], sems.at[c]))
    return made


def ahead(copies, depth=2):
    start_all(copies[:depth])

    def wait(i):
        copies[i].wait()
        start_all(copies[i + depth : i + depth + 1])

    return wait


def sent_columns(held, pairs, sems, group, chunk, steps):
    size = pairs[0].shape[0]
    first, end = group * steps // sems.shape[0], (group + 1) * steps // sems.shape[0]
    part = pl.ds(first * chunk, (end - first) * chunk)
    return [
        pltpu.make_async_copy(
            held.at[pl.ds(i * size, size), part], pair.at[:, part], sems.at[group, i]
        )
        for i, pair in enumerate(pairs)
    ]


def start_all(copies):
    for copy in copies:
        copy.start()


def wait_all(copies):
    for copy in copies:
        copy.wait()


def activation(joined, half):
    gate, up = joined[:, :half], joined[:, half:]
    return (gate * jax.nn.sigmoid(gate) * up).astype(BF16)


def middle_grad(joined, act_grad, half):
    gate, up = joined[:, :half], joined[:, half:]
    sigmoid_gate = jax.nn.sigmoid(gate)
    gate_grad = act_grad * up * sigmoid_gate * (1.0 + gate * (1.0 - sigmoid_gate))
    up_grad = act_grad * gate * sigmoid_gate
    return jnp.concatenate([gate_grad, up_grad], axis=1).astype(BF16)


def back_rows(mid, held_in, held, back, sems, chunk, steps, before=None):
    groups = sems.shape[0]
    done = []
    for c in range(steps):
        if before is not None:
            before(c)
        part = columns(c, chunk)
        held[:, part] = dot(mid, held_in[part, :], 1, 1).astype(BF16)
        if (c + 1) * groups // steps > c * groups // steps:
            group = (c + 1) * groups // steps - 1
            copies = sent_columns(held, back, sems, group, chunk, steps)
            start_all(copies)
            done += copies
    wait_all(done)


def forward_kernel(arrays, places, inward, outward):
    count, halves, rows = len(arrays), len(places), len(places) // 2 * arrays[0].shape[0]
    features, inner = inward.shape
    half = outward.shape[0]
    chunk = min(CHUNK, features)
    steps = features // chunk
    groups = min(GROUPS, steps)

    def body(*refs):
        given, (w_in, w_out), refs = refs[:count], refs[count : count + 2], refs[count + 2 :]
        (joined, active), partial = refs[:2], refs[2 : 2 + halves // 2]
        x, held_in, held_out, out, x_sems, in_sems, out_sems, done_sems = refs[2 + halves // 2 :]
        x_copies = row_copies(given, places, x, x_sems)
        start_all(x_copies)
        wait_weight = ahead(
            weight_copies(w_in, held_in, in_sems, chunk, True)
            + weight_copies(w_out, held_out, out_sems, chunk, False)
        )
        wait_all(x_copies)
        total = jnp.zeros((rows, inner), F32)
        for c in range(steps):
            wait_weight(c)
            total = total + dot(x[:, columns(c, chunk)], held_in[columns(c, chunk), :])
        joined[...] = total
        act = activation(total, half)
        active[...] = act
        done = []
        for c in range(steps):
            wait_weight(steps + c)
            out[:, columns(c, chunk)] = dot(act, held_out[:, columns(c, chunk)]).astype(BF16)
            if (c + 1) * groups // steps > c * groups // steps:
                group = (c + 1) * groups // steps - 1
                copies = sent_columns(out, partial, done_sems, group, chunk, steps)
                start_all(copies)
                done += copies
        wait_all(done)

    pair = jax.ShapeDtypeStruct((2 * rows // halves, features), BF16)
    results = pl.pallas_call(
        body,
        in_specs=[ANYWHERE] * (count + 2),
        out_specs=[IN_VMEM] * 2 + [ANYWHERE] * (halves // 2),
        out_shape=[
            jax.ShapeDtypeStruct((rows, inner), F32),
            jax.ShapeDtypeStruct((rows, half), BF16),
        ]
        + [pair] * (halves // 2),
        scratch_shapes=[
            pltpu.VMEM((rows, features), BF16),
            pltpu.VMEM((features, inner), BF16),
            pltpu.VMEM((half, features), BF16),
            pltpu.VMEM((rows, features), BF16),
            pltpu.SemaphoreType.DMA((halves,)),
            pltpu.SemaphoreType.DMA((steps,)),
            pltpu.SemaphoreType.DMA((steps,)),
            pltpu.SemaphoreType.DMA((groups, halves // 2)),
        ],
        compiler_params=params(),
        cost_estimate=pl.CostEstimate(
            flops=6 * rows * features * half, bytes_accessed=16 * MIB, transcendentals=0
        ),
        name="expert_forward",
    )(*arrays, inward, outward)
    return results[0], results[1], results[2:]


def act_grad_kernel(arrays, places, outward):
    count, halves, rows = len(arrays), len(places), len(places) // 2 * arrays[0].shape[0]
    half, features = outward.shape
    chunk = min(CHUNK, features)
    steps = features // chunk

    def body(*refs):
        given, w_out, out, s, held_out, s_sems, out_sems = refs[:count], *refs[count:]
        s_copies = row_copies(given, places, s, s_sems)
        start_all(s_copies)
        wait_weight = ahead(weight_copies(w_out, held_out, out_sems, chunk, False))
        wait_all(s_copies)
        act_grad = jnp.zeros((rows, half), F32)
        for c in range(steps):
            wait_weight(c)
            part = columns(c, chunk)
            act_grad = act_grad + dot(s[:, part], held_out[:, part], 1, 1)
        out[...] = act_grad

    return pl.pallas_call(
        body,
        in_specs=[ANYWHERE] * (count + 1),
        out_specs=IN_VMEM,
        out_shape=jax.ShapeDtypeStruct((rows, half), F32),
        scratch_shapes=[
            pltpu.VMEM((rows, features), BF16),
            pltpu.VMEM((half, features), BF16),
            pltpu.SemaphoreType.DMA((halves,)),
            pltpu.SemaphoreType.DMA((steps,)),
        ],
        compiler_params=params(),
        cost_estimate=pl.CostEstimate(
            flops=2 * rows * features * half, bytes_accessed=8 * MIB, transcendentals=0
        ),
        name="act_grads",
    )(*arrays, outward)


def draft_backward_kernel(arrays, places, act_grads, inward):
    count, halves, rows = len(arrays), len(places), len(places) // 2 * arrays[0].shape[0]
    features, inner = inward.shape
    half = inner // 2
    chunk = min(CHUNK, features)
    steps = features // chunk
    groups = min(GROUPS, steps)

    def body(*refs):
        given, (act_grad, w_in, middle, active), refs = (
            refs[:count], refs[count : count + 4], refs[count + 4 :],
        )
        back, (x, held_in, x_sems, in_sems, done_sems) = refs[:-5], refs[-5:]
        x_copies = row_copies(given, places, x, x_sems)
        start_all(x_copies)
        wait_weight = ahead(weight_copies(w_in, held_in, in_sems, chunk, True))
        wait_all(x_copies)
        total = jnp.zeros((rows, inner), F32)
        for c in range(steps):
            wait_weight(c)
            total = total + dot(x[:, columns(c, chunk)], held_in[columns(c, chunk), :])
        active[...] = activation(total, half)
        middle[...] = middle_grad(total, act_grad[...], half)
        back_rows(middle[...], held_in, x, back, done_sems, chunk, steps)

    results = pl.pallas_call(
        body,
        in_specs=[ANYWHERE] * count + [IN_VMEM, ANYWHERE],
        out_specs=[IN_VMEM] * 2 + [ANYWHERE] * (halves // 2),
        out_shape=[
            jax.ShapeDtypeStruct((rows, inner), BF16),
            jax.ShapeDtypeStruct((rows, half), BF16),
        ]
        + [jax.ShapeDtypeStruct((2 * rows // halves, features), BF16)] * (halves // 2),
        scratch_shapes=[
            pltpu.VMEM((rows, features), BF16),
            pltpu.VMEM((features, inner), BF16),
            pltpu.SemaphoreType.DMA((halves,)),
            pltpu.SemaphoreType.DMA((steps,)),
            pltpu.SemaphoreType.DMA((groups, halves // 2)),
        ],
        compiler_params=params(),
        cost_estimate=pl.CostEstimate(
            flops=4 * rows * features * inner, bytes_accessed=12 * MIB, transcendentals=0
        ),
        name="draft_backward",
    )(*arrays, act_grads, inward)
    return results[0], results[1], results[2:]


def main_backward_kernel(arrays, places, joined, inward, outward):
    count, halves, rows = len(arrays), len(places), len(places) // 2 * arrays[0].shape[0]
    features, inner = inward.shape
    half = outward.shape[0]
    chunk = min(CHUNK, features)
    steps = features // chunk
    groups = min(GROUPS, steps)

    def body(*refs):
        given, (joined, w_in, w_out, middle), refs = (
            refs[:count], refs[count : count + 4], refs[count + 4 :],
        )
        back, (s, held_in, held_out, s_sems, in_sems, out_sems, done_sems) = refs[:-7], refs[-7:]
        s_copies = row_copies(given, places, s, s_sems)
        start_all(s_copies)
        wait_weight = ahead(
            weight_copies(w_out, held_out, out_sems, chunk, False)
            + weight_copies(w_in, held_in, in_sems, chunk, True)
        )
        wait_all(s_copies)
        act_grad = jnp.zeros((rows, half), F32)
        for c in range(steps):
            wait_weight(c)
            part = columns(c, chunk)
            act_grad = act_grad + dot(s[:, part], held_out[:, part], 1, 1)
        middle[...] = middle_grad(joined[...], act_grad, half)
        back_rows(
            middle[...], held_in, s, back, done_sems, chunk, steps, lambda c: wait_weight(steps + c)
        )

    results = pl.pallas_call(
        body,
        in_specs=[ANYWHERE] * count + [IN_VMEM] + [ANYWHERE] * 2,
        out_specs=[IN_VMEM] + [ANYWHERE] * (halves // 2),
        out_shape=[jax.ShapeDtypeStruct((rows, inner), BF16)]
        + [jax.ShapeDtypeStruct((2 * rows // halves, features), BF16)] * (halves // 2),
        scratch_shapes=[
            pltpu.VMEM((rows, features), BF16),
            pltpu.VMEM((features, inner), BF16),
            pltpu.VMEM((half, features), BF16),
            pltpu.SemaphoreType.DMA((halves,)),
            pltpu.SemaphoreType.DMA((steps,)),
            pltpu.SemaphoreType.DMA((steps,)),
            pltpu.SemaphoreType.DMA((groups, halves // 2)),
        ],
        compiler_params=params(),
        cost_estimate=pl.CostEstimate(
            flops=6 * rows * features * half, bytes_accessed=16 * MIB, transcendentals=0
        ),
        name="main_backward",
    )(*arrays, joined, inward, outward)
    return results[0], results[1:]


def weight_grad_kernel(is_draft, first, second, third, places, middles, actives):
    main_places, draft_places = places
    count, halves, rows = len(first), len(main_places), len(main_places) // 2 * first[0].shape[0]
    features = first[0].shape[1]
    inner, half = middles[0].shape[1], actives[0].shape[1]
    chunk = min(CHUNK, features)
    steps = features // chunk

    def body(flag, *refs):
        one, two, three = refs[:count], refs[count : 2 * count], refs[2 * count : 3 * count]
        main_mid, draft_mid, main_act, draft_act, in_grad, out_grad = refs[
            3 * count : 3 * count + 6
        ]
        x, s, mid, act, in_held, out_held, x_sems, s_sems, in_sems, out_sems = refs[3 * count + 6 :]
        draft = flag[0] == 1

        @pl.when(draft)
        def _():
            start_all(row_copies(two, draft_places, x, x_sems) + row_copies(one, draft_places, s, s_sems))
            mid[...] = draft_mid[...]
            act[...] = draft_act[...]

        @pl.when(jnp.logical_not(draft))
        def _():
            start_all(row_copies(one, main_places, x, x_sems) + row_copies(three, main_places, s, s_sems))
            mid[...] = main_mid[...]
            act[...] = main_act[...]

        wait_all(row_copies(one, main_places, x, x_sems))
        in_copies, out_copies = [], []
        for c in range(steps):
            part = columns(c, chunk)
            in_held[part, :] = dot(x[:, part], mid[...], 0, 0).astype(BF16)
            copy = pltpu.make_async_copy(in_held.at[part, :], in_grad.at[0, part, :], in_sems.at[c])
            copy.start()
            in_copies.append(copy)
        wait_all(row_copies(one, main_places, s, s_sems))
        for c in range(steps):
            part = columns(c, chunk)
            out_held[:, part] = dot(act[...], s[:, part], 0, 0).astype(BF16)
            copy = pltpu.make_async_copy(
                out_held.at[:, part], out_grad.at[0, :, part], out_sems.at[c]
            )
            copy.start()
            out_copies.append(copy)
        wait_all(in_copies + out_copies)

    return pl.pallas_call(
        body,
        in_specs=[pl.BlockSpec(memory_space=pltpu.SMEM)]
        + [ANYWHERE] * (3 * count)
        + [IN_VMEM] * 4,
        out_specs=[ANYWHERE] * 2,
        out_shape=[
            jax.ShapeDtypeStruct((1, features, inner), BF16),
            jax.ShapeDtypeStruct((1, half, features), BF16),
        ],
        scratch_shapes=[
            pltpu.VMEM((rows, features), BF16),
            pltpu.VMEM((rows, features), BF16),
            pltpu.VMEM((rows, inner), BF16),
            pltpu.VMEM((rows, half), BF16),
            pltpu.VMEM((features, inner), BF16),
            pltpu.VMEM((half, features), BF16),
            pltpu.SemaphoreType.DMA((halves,)),
            pltpu.SemaphoreType.DMA((halves,)),
            pltpu.SemaphoreType.DMA((steps,)),
            pltpu.SemaphoreType.DMA((steps,)),
        ],
        compiler_params=params(),
        cost_estimate=pl.CostEstimate(
            flops=6 * rows * features * half, bytes_accessed=16 * MIB, transcendentals=0
        ),
        name="weight_grads",
    )(is_draft, *first, *second, *third, *middles, *actives)


def on_device(
    hidden_rows,
    embed_rows,
    gain_hidden,
    gain_embed,
    main_route,
    main_gates,
    draft_route,
    draft_gates,
    draft_cotangent,
    expert_in,
    expert_out,
):
    groups, per_group = SIZES[:2]
    counts = ((groups - 1) * per_group * CAP, groups * per_group * CAP)
    inward = expert_in[0]
    outward = expert_out[0]
    gain_hidden = gain_hidden[None]
    gain_embed = gain_embed[None]
    is_draft = (lax.axis_index("g") == groups - 1).astype(jnp.int32)[None]

    send, mixing, picked_mixing, weight, table = tables(
        main_route.T, main_gates.T, draft_route.T, draft_gates.T, hidden_rows, draft_cotangent,
        counts,
    )
    first, _ = plane_gather(flat(exchange(send)), False)
    joined, main_active, partial = forward_kernel(first, PAIRS, inward, outward)
    main_sum, (picked_hidden, picked_embed, picked_cotangent) = plane_sum(
        partial, False, lambda: pick_kernel(table, hidden_rows, embed_rows, draft_cotangent)
    )
    main_total = exchange(main_sum)

    draft_rows = draft_row_kernel(
        picked_hidden, picked_embed, picked_mixing, weight, main_total, gain_hidden, gain_embed,
        counts,
    )
    second, draft_act_grad = plane_gather(
        flat(exchange(draft_rows)), True, lambda: act_grad_kernel(first, PLAIN, outward)
    )
    draft_mid, draft_active, draft_back = draft_backward_kernel(
        second, PLAIN, draft_act_grad, inward
    )
    draft_total = exchange(plane_sum_direct(draft_back, True))

    signal = main_signal_kernel(
        picked_hidden, picked_cotangent, picked_mixing, weight, main_total, draft_total,
        gain_hidden, counts,
    )
    third, _ = plane_gather(flat(exchange(signal)), False)
    main_mid, main_back = main_backward_kernel(third, PAIRS, joined, inward, outward)
    token_args = (
        hidden_rows, embed_rows, draft_cotangent, mixing, main_total, draft_total, gain_hidden,
        gain_embed, counts,
    )
    back_sum, (settled_grad, embed_grad) = plane_sum(
        main_back,
        False,
        lambda: token_grad_kernel(*token_args),
        lambda early: token_grad_kernel(*token_args, earlier=early),
    )
    back_total = exchange(back_sum)
    in_grad, out_grad = weight_grad_kernel(
        is_draft, first, second, third, (PAIRS, PLAIN), (main_mid, draft_mid),
        (main_active, draft_active),
    )
    hidden_grad = hidden_grad_kernel(settled_grad, mixing, back_total, counts)
    return (hidden_grad, embed_grad, in_grad, out_grad)


def solution(mesh):
    fine = Mesh(mesh.devices.reshape(SIZES), AXES)
    rows = P(AXES, None)
    blocks = P(AXES, None, None)
    return jax.shard_map(
        on_device,
        mesh=fine,
        in_specs=(rows, rows, P(), P(), rows, rows, rows, rows, rows, blocks, blocks),
        out_specs=(rows, rows, blocks, blocks),
        check_vma=False,
    )
```

```python
import functools
import itertools

import jax
import jax.numpy as jnp
from jax import lax
from jax.experimental import pallas as pl
from jax.experimental.pallas import tpu as pltpu
from jax.sharding import Mesh, PartitionSpec as P

CAP = 2
EPSILON = 1e-06
BF16 = jnp.bfloat16
F32 = jnp.float32
AXES = ("g", "z", "y", "x")
SIZES = (4, 4, 4, 2)
LANES = 128
CHUNK = 1792
MIB = 1024 * 1024
GROUPS = 4
IN_VMEM = pl.BlockSpec(memory_space=pltpu.VMEM)
ANYWHERE = pl.BlockSpec(memory_space=pl.ANY)
IN_SMEM = pl.BlockSpec(memory_space=pltpu.SMEM)


def mover(draft_only, dy, dx):
    groups, depth, tall, wide = SIZES

    def number(g, z, y, x):
        return ((g * depth + z) * tall + y) * wide + x

    def target(g, z, y, x):
        if not draft_only or g == groups - 1:
            return number(g, z, (y + dy) % tall, x ^ dx)
        if dx:
            return number(g, (z + 1) % depth, y, x) if g == 1 else number(2 - g, z, y, x ^ 1)
        return number(g ^ 1, z, y, x) if g < 2 else number(g, (z + dy) % depth, y, x)

    places = itertools.product(*map(range, SIZES))
    pairs = [(number(*place), target(*place)) for place in places]
    return lambda values: lax.ppermute(values, AXES, pairs)


def movers(draft_only):
    return mover(draft_only, 1, 0), mover(draft_only, -1, 0), mover(draft_only, 0, 1)


def plane_gather(rows, draft_only, beside=None):
    up, down, cross = movers(draft_only)
    half = rows.shape[0] // 2
    below, above, other = up(rows), down(rows), cross(rows)
    made = None
    if beside is not None:
        (below, above, other), made = lax.optimization_barrier(((below, above, other), beside()))
    far = up(below)
    b_other = other[half:]
    b_other_below, b_other_above = up(b_other), down(b_other)
    a_other_below, a_other_above = cross(below[:half]), cross(above[:half])
    a_other_far, b_other_far = cross(far[:half]), down(b_other_above)
    arrays = [
        rows, below, above, other, far, b_other_below, b_other_above, b_other_far, a_other_below,
        a_other_above, a_other_far,
    ]
    return arrays, made


PLACES = ((0, 0), (-1, 0), (1, 0), (0, 1), (2, 0), (-1, 1), (1, 1), (2, 1))
PLAIN = (
    (0, 0), (0, 1), (1, 0), (1, 1), (2, 0), (2, 1), (3, 0), (3, 1),
    (4, 0), (4, 1), (8, 0), (5, 0), (9, 0), (6, 0), (10, 0), (7, 0),
)
PAIRS = (
    (4, 1), (6, 0), (7, 0), (1, 1), (10, 0), (8, 0), (9, 0), (3, 0),
    (2, 1), (4, 0), (5, 0), (1, 0), (2, 0), (3, 1), (0, 0), (0, 1),
)


def plane_sum_direct(partials, draft_only):
    sent = [
        mover(draft_only, dy, dx)(partial)
        for (dy, dx), partial in reversed(list(zip(PLACES, partials))[1:])
    ]

    def body(*refs):
        total = wide(refs[0][...])
        for ref in refs[1:-1]:
            total = total + wide(ref[...])
        refs[-1][...] = paired(total.astype(BF16))

    size = partials[0].shape[0]
    return adder(body, "sums_direct", [partials[0], *sent], [(size // CAP, CAP)])[0]


def wide(values):
    return values.astype(F32)


def adder(body, name, inputs, results):
    features = inputs[0].shape[1]
    return pl.pallas_call(
        body,
        in_specs=[IN_VMEM] * len(inputs),
        out_specs=[IN_VMEM] * len(results),
        out_shape=[jax.ShapeDtypeStruct((*n, features), BF16) for n in results],
        compiler_params=params(8),
        name=name,
    )(*inputs)


def plane_sum(partials, draft_only, beside=None, beside_next=None):
    up, down, cross = movers(draft_only)
    up_first, down_first, cross_first, cross_second, up_next, down_next, last, own = partials
    half = own.shape[0] // 2
    low, high = slice(0, half), slice(half, 2 * half)

    def second(up_had, down_had, from_up, from_down, from_cross, up_out, down_out):
        up_out[low] = (wide(up_had[low]) + wide(from_up[low])).astype(BF16)
        up_out[high] = (wide(up_had[high]) + wide(from_cross[low])).astype(BF16)
        down_out[low] = (wide(down_had[low]) + wide(from_down[low])).astype(BF16)
        down_out[high] = (wide(down_had[high]) + wide(from_cross[high])).astype(BF16)

    def third(had, up_one, down_two, up_two, cross_two, a_out, b_out):
        a_out[...] = (wide(had[low]) + wide(cross_two[low]) + wide(up_two[high])).astype(BF16)
        b_out[...] = (wide(had[high]) + wide(up_one[high]) + wide(down_two[low])).astype(BF16)

    def fourth(had, down_one, down_two, up_two, cross_two, a_last, b_last, out):
        a_total = wide(had[low]) + wide(cross_two[high]) + wide(down_two[high]) + wide(a_last[...])
        b_total = wide(had[high]) + wide(down_one[high]) + wide(up_two[low]) + wide(b_last[...])
        out[: half // CAP] = paired(a_total.astype(BF16))
        out[half // CAP :] = paired(b_total.astype(BF16))

    up_one, down_one, cross_one = up(up_first), down(down_first), cross(cross_first)
    made = None
    if beside is not None:
        (up_one, down_one, cross_one), made = lax.optimization_barrier(
            ((up_one, down_one, cross_one), beside())
        )
    up_send, down_send = adder(
        second, "sums_second", [up_next, down_next, up_one, down_one, cross_one], [(2 * half,)] * 2
    )
    up_send, down_send, cross_second = lax.optimization_barrier((up_send, down_send, cross_second))
    up_two, down_two, cross_two = up(up_send), down(down_send), cross(cross_second)
    if beside_next is not None:
        (up_two, down_two, cross_two), made = lax.optimization_barrier(
            ((up_two, down_two, cross_two), beside_next(made))
        )
    a_send, b_send = adder(
        third, "sums_third", [last, up_one, down_two, up_two, cross_two], [(half,)] * 2
    )
    (total,) = adder(
        fourth,
        "sums_fourth",
        [own, down_one, down_two, up_two, cross_two, up(a_send), cross(b_send)],
        [(2 * half // CAP, CAP)],
    )
    return total, made


def exchange(rows):
    return lax.all_to_all(rows, ("g", "z"), 0, 0, tiled=True)


def flat(pairs):
    return pairs.reshape(-1, pairs.shape[-1])


def paired(rows):
    return rows.reshape(-1, CAP, rows.shape[-1])


def params(mebibytes=60):
    return pltpu.CompilerParams(vmem_limit_bytes=mebibytes * MIB)


def dot(left, right, over_left=1, over_right=0):
    return lax.dot_general(
        left, right, (((over_left,), (over_right,)), ((), ())), preferred_element_type=F32
    )


def split_three(values):
    high = values.astype(BF16)
    rest = values - high.astype(F32)
    middle = rest.astype(BF16)
    return (high, middle, (rest - middle.astype(F32)).astype(BF16))


def weighted(mixing, rows):
    parts = jnp.concatenate(split_three(mixing), axis=1)
    return dot(parts, jnp.concatenate([rows] * 3, axis=0))


def inverse_rms(values):
    return lax.rsqrt(jnp.mean(values * values, axis=-1, keepdims=True) + EPSILON)


def norm_backward(values, inverse, scaled):
    mean = jnp.mean(values * scaled, axis=-1, keepdims=True)
    return inverse * scaled - values * (inverse * inverse * inverse * mean)


def tables(main_route, main_gates, draft_route, draft_gates, hidden, cotangent, counts):
    main_slots, slots = counts
    tokens, features = hidden.shape
    chunk = features // 2

    def body(mr, mg, dr, dg, hid, cot, send, mix, picked, weight, table):
        @pl.when(pl.program_id(0) == 0)
        def _():
            slot = lax.broadcasted_iota(jnp.int32, (slots, tokens), 0)
            is_main = slot < main_slots
            label = jnp.where(is_main, slot, slot - main_slots) // CAP
            held = jnp.zeros((slots, tokens), F32)
            gates = jnp.zeros((slots, tokens), F32)
            for k in range(mr.shape[0]):
                one = slice(k, k + 1)
                hit = jnp.where(is_main, mr[one, :], dr[one, :]) == label
                held = jnp.where(hit, 1.0, held)
                gates = jnp.where(hit, jnp.where(is_main, mg[one, :], dg[one, :]), gates)
            row = lax.broadcasted_iota(jnp.int32, (tokens, tokens), 0)
            column = lax.broadcasted_iota(jnp.int32, (tokens, tokens), 1)
            before = jnp.where(row < column, 1.0, 0.0).astype(BF16)
            rank = dot(held.astype(BF16), before)
            kept = (held > 0.5) & (rank == (slot % CAP).astype(F32))
            slot_mixing = jnp.where(kept, gates, 0.0)
            chosen = jnp.where(kept, 1.0, 0.0).astype(BF16)
            spare = jnp.zeros((LANES - slots, tokens), F32)
            mixing = jnp.concatenate([slot_mixing, spare], axis=0).T
            mix[...] = mixing
            table[...] = chosen
            high, middle, low = split_three(mixing)
            picked[...] = dot(chosen, high) + dot(chosen, middle) + dot(chosen, low)
            sums = jnp.sum(slot_mixing, axis=1, keepdims=True)
            weight[...] = jnp.broadcast_to(sums, (slots, LANES))

        chosen = table[...]
        hidden_part = dot(chosen, hid[...])
        cotangent_part = dot(chosen, cot[...])
        slot = lax.broadcasted_iota(jnp.int32, (slots, chunk), 0)
        rows = jnp.where(slot < main_slots, hidden_part, weight[:, :1] * cotangent_part)
        send[...] = paired(rows.astype(BF16))

    whole = pl.BlockSpec(main_route.shape, lambda i: (0, 0))
    wide = pl.BlockSpec((tokens, chunk), lambda i: (0, i))
    slim = pl.BlockSpec((slots // CAP, CAP, chunk), lambda i: (0, 0, i))
    small = jax.ShapeDtypeStruct((slots, LANES), F32)
    small_spec = pl.BlockSpec((slots, LANES), lambda i: (0, 0))
    return pl.pallas_call(
        body,
        grid=(features // chunk,),
        in_specs=[whole] * 4 + [wide] * 2,
        out_specs=[
            slim,
            pl.BlockSpec((tokens, LANES), lambda i: (0, 0)),
            small_spec,
            small_spec,
            pl.BlockSpec((slots, tokens), lambda i: (0, 0)),
        ],
        out_shape=[
            jax.ShapeDtypeStruct((slots // CAP, CAP, features), BF16),
            jax.ShapeDtypeStruct((tokens, LANES), F32),
            small,
            small,
            jax.ShapeDtypeStruct((slots, tokens), BF16),
        ],
        compiler_params=params(),
        name="slot_tables",
    )(main_route, main_gates, draft_route, draft_gates, hidden, cotangent)


def pick_kernel(table, hidden, embed, cotangent):
    slots, tokens = table.shape
    features = hidden.shape[1]
    chunk = features // 2

    def body(table, *refs):
        chosen = table[...]
        for source, out in zip(refs[:3], refs[3:]):
            out[...] = dot(chosen, source[...]).astype(BF16)

    wide = pl.BlockSpec((tokens, chunk), lambda i: (0, i))
    slim = pl.BlockSpec((slots, chunk), lambda i: (0, i))
    return pl.pallas_call(
        body,
        grid=(features // chunk,),
        in_specs=[pl.BlockSpec((slots, tokens), lambda i: (0, 0))] + [wide] * 3,
        out_specs=[slim] * 3,
        out_shape=[jax.ShapeDtypeStruct((slots, features), BF16)] * 3,
        compiler_params=params(),
        cost_estimate=pl.CostEstimate(
            flops=6 * slots * tokens * features, bytes_accessed=8 * MIB, transcendentals=0
        ),
        name="slot_rows",
    )(table, hidden, embed, cotangent)


def lane_part(values, low, high):
    lane = lax.broadcasted_iota(jnp.int32, values.shape, 1)
    return jnp.where((lane >= low) & (lane < high), values, 0.0)


def row_part(values, low, high):
    row = lax.broadcasted_iota(jnp.int32, values.shape, 0)
    return jnp.where((row >= low) & (row < high), values, jnp.zeros_like(values))


def whole(array):
    return pl.BlockSpec(array.shape, lambda i: (0,) * array.ndim)


def draft_row_kernel(hp, ep, picked, weight, main_total, gain_hidden, gain_embed, counts):
    main_slots, slots = counts

    def body(hp, ep, picked, weight, total, gain_h, gain_e, out):
        mixing = lane_part(picked[:, :slots], 0, main_slots)
        settled = hp[...].astype(F32) + weighted(mixing, flat(total[...]))
        embedded = ep[...].astype(F32)
        joined = (
            settled * inverse_rms(settled) * gain_h[...]
            + embedded * inverse_rms(embedded) * gain_e[...]
        )
        joined = jnp.where(weight[:, :1] > 0.0, joined, 0.0)
        out[...] = paired(row_part(joined, main_slots, slots).astype(BF16))

    given = (hp, ep, picked, weight, main_total, gain_hidden, gain_embed)
    return pl.pallas_call(
        body,
        grid=(1,),
        in_specs=[whole(v) for v in given],
        out_specs=whole(main_total),
        out_shape=jax.ShapeDtypeStruct(main_total.shape, BF16),
        compiler_params=params(),
        name="draft_rows",
    )(*given)


def main_signal_kernel(hp, cp, picked, weight, main_total, draft_total, gain_hidden, counts):
    main_slots, slots = counts

    def body(hp, cp, picked, weight, total, drafts, gain_h, out):
        mixing = picked[:, :slots]
        settled = hp[...].astype(F32) + weighted(
            lane_part(mixing, 0, main_slots), flat(total[...])
        )
        lifted = cp[...].astype(F32) + weighted(
            lane_part(mixing, main_slots, slots), flat(drafts[...])
        )
        grad = norm_backward(settled, inverse_rms(settled), gain_h[...] * lifted)
        out[...] = paired(row_part(weight[:, :1] * grad, 0, main_slots).astype(BF16))

    given = (hp, cp, picked, weight, main_total, draft_total, gain_hidden)
    return pl.pallas_call(
        body,
        grid=(1,),
        in_specs=[whole(v) for v in given],
        out_specs=whole(main_total),
        out_shape=jax.ShapeDtypeStruct(main_total.shape, BF16),
        compiler_params=params(),
        name="main_signals",
    )(*given)


def token_grad_kernel(
    hidden, embed, cotangent, mixing, main_total, draft_total, gain_hidden, gain_embed, counts,
    earlier=None,
):
    main_slots, slots = counts
    tokens, features = hidden.shape
    block = 16
    steps = tokens // block // 2
    first = 0 if earlier is None else steps
    held = () if earlier is None else tuple(earlier)

    def body(hid, emb, cot, mix, total, drafts, gain_h, gain_e, *refs):
        settled_grad, embed_grad = refs[-2:]
        mixed = mix[:, :slots]
        settled = hid[...].astype(F32) + weighted(
            lane_part(mixed, 0, main_slots), flat(total[...])
        )
        lifted = cot[...].astype(F32) + weighted(
            lane_part(mixed, main_slots, slots), flat(drafts[...])
        )
        settled_grad[...] = norm_backward(settled, inverse_rms(settled), gain_h[...] * lifted)
        embedded = emb[...].astype(F32)
        embed_grad[...] = norm_backward(
            embedded, inverse_rms(embedded), gain_e[...] * lifted
        ).astype(BF16)

    wide = pl.BlockSpec((block, features), lambda i: (first + i, 0))
    slim = pl.BlockSpec((slots // CAP, CAP, features), lambda i: (0, 0, 0))
    gain = pl.BlockSpec((1, features), lambda i: (0, 0))
    return pl.pallas_call(
        body,
        grid=(steps,),
        in_specs=[wide] * 3
        + [pl.BlockSpec((block, LANES), lambda i: (first + i, 0))]
        + [slim] * 2
        + [gain] * 2
        + [ANYWHERE] * len(held),
        input_output_aliases={8 + k: k for k in range(len(held))},
        out_specs=[wide] * 2,
        out_shape=[
            jax.ShapeDtypeStruct(hidden.shape, F32),
            jax.ShapeDtypeStruct(hidden.shape, BF16),
        ],
        compiler_params=params(),
        cost_estimate=pl.CostEstimate(
            flops=tokens * features * 50, bytes_accessed=6 * tokens * features, transcendentals=0
        ),
        name="token_grads",
    )(hidden, embed, cotangent, mixing, main_total, draft_total, gain_hidden, gain_embed, *held)


def hidden_grad_kernel(settled_grad, mixing, back_total, counts):
    main_slots, slots = counts
    tokens, features = settled_grad.shape
    chunk = features // 2

    def body(grad, mix, total, out):
        mixed = lane_part(mix[:, :slots], 0, main_slots)
        out[...] = (
            grad[...] + weighted(mixed, flat(total[...]))
        ).astype(BF16)

    wide = pl.BlockSpec((tokens, chunk), lambda i: (0, i))
    return pl.pallas_call(
        body,
        grid=(features // chunk,),
        in_specs=[
            wide,
            pl.BlockSpec((tokens, LANES), lambda i: (0, 0)),
            pl.BlockSpec((slots // CAP, CAP, chunk), lambda i: (0, 0, i)),
        ],
        out_specs=wide,
        out_shape=jax.ShapeDtypeStruct(settled_grad.shape, BF16),
        compiler_params=params(),
        name="hidden_grads",
    )(settled_grad, mixing, back_total)


def columns(index, chunk):
    return pl.ds(index * chunk, chunk)


def row_copies(arrays, places, held, sems):
    size = held.shape[0] // len(places)
    return [
        pltpu.make_async_copy(
            arrays[which].at[pl.ds(half * size, size), :],
            held.at[pl.ds(i * size, size), :],
            sems.at[i],
        )
        for i, (which, half) in enumerate(places)
    ]


def weight_copies(whole, held, sems, chunk, over_rows):
    made = []
    for c in range(sems.shape[0]):
        place = (columns(c, chunk), slice(None)) if over_rows else (slice(None), columns(c, chunk))
        made.append(pltpu.make_async_copy(whole.at[place], held.at[place], sems.at[c]))
    return made


def ahead(copies, depth=2):
    start_all(copies[:depth])

    def wait(i):
        copies[i].wait()
        start_all(copies[i + depth : i + depth + 1])

    return wait


def sent_columns(held, pairs, sems, group, chunk, steps):
    size = pairs[0].shape[0]
    first, end = group * steps // sems.shape[0], (group + 1) * steps // sems.shape[0]
    part = pl.ds(first * chunk, (end - first) * chunk)
    return [
        pltpu.make_async_copy(
            held.at[pl.ds(i * size, size), part], pair.at[:, part], sems.at[group, i]
        )
        for i, pair in enumerate(pairs)
    ]


def start_all(copies):
    for copy in copies:
        copy.start()


def wait_all(copies):
    for copy in copies:
        copy.wait()


def activation(joined, half):
    gate, up = joined[:, :half], joined[:, half:]
    return (gate * jax.nn.sigmoid(gate) * up).astype(BF16)


def middle_grad(joined, act_grad, half):
    gate, up = joined[:, :half], joined[:, half:]
    sigmoid_gate = jax.nn.sigmoid(gate)
    gate_grad = act_grad * up * sigmoid_gate * (1.0 + gate * (1.0 - sigmoid_gate))
    up_grad = act_grad * gate * sigmoid_gate
    return jnp.concatenate([gate_grad, up_grad], axis=1).astype(BF16)


def back_rows(mid, held_in, held, back, sems, chunk, steps, before=None):
    groups = sems.shape[0]
    done = []
    for c in range(steps):
        if before is not None:
            before(c)
        part = columns(c, chunk)
        held[:, part] = dot(mid, held_in[part, :], 1, 1).astype(BF16)
        if (c + 1) * groups // steps > c * groups // steps:
            group = (c + 1) * groups // steps - 1
            copies = sent_columns(held, back, sems, group, chunk, steps)
            start_all(copies)
            done += copies
    wait_all(done)


def forward_kernel(arrays, places, inward, outward):
    count, halves, rows = len(arrays), len(places), len(places) // 2 * arrays[0].shape[0]
    features, inner = inward.shape
    half = outward.shape[0]
    chunk = min(CHUNK, features)
    steps = features // chunk
    groups = min(GROUPS, steps)

    def body(*refs):
        given, (w_in, w_out), refs = refs[:count], refs[count : count + 2], refs[count + 2 :]
        (joined, active), partial = refs[:2], refs[2 : 2 + halves // 2]
        x, held_in, held_out, out, x_sems, in_sems, out_sems, done_sems = refs[2 + halves // 2 :]
        x_copies = row_copies(given, places, x, x_sems)
        start_all(x_copies)
        wait_weight = ahead(
            weight_copies(w_in, held_in, in_sems, chunk, True)
            + weight_copies(w_out, held_out, out_sems, chunk, False)
        )
        wait_all(x_copies)
        total = jnp.zeros((rows, inner), F32)
        for c in range(steps):
            wait_weight(c)
            total = total + dot(x[:, columns(c, chunk)], held_in[columns(c, chunk), :])
        joined[...] = total
        act = activation(total, half)
        active[...] = act
        done = []
        for c in range(steps):
            wait_weight(steps + c)
            out[:, columns(c, chunk)] = dot(act, held_out[:, columns(c, chunk)]).astype(BF16)
            if (c + 1) * groups // steps > c * groups // steps:
                group = (c + 1) * groups // steps - 1
                copies = sent_columns(out, partial, done_sems, group, chunk, steps)
                start_all(copies)
                done += copies
        wait_all(done)

    pair = jax.ShapeDtypeStruct((2 * rows // halves, features), BF16)
    results = pl.pallas_call(
        body,
        in_specs=[ANYWHERE] * (count + 2),
        out_specs=[IN_VMEM] * 2 + [ANYWHERE] * (halves // 2),
        out_shape=[
            jax.ShapeDtypeStruct((rows, inner), F32),
            jax.ShapeDtypeStruct((rows, half), BF16),
        ]
        + [pair] * (halves // 2),
        scratch_shapes=[
            pltpu.VMEM((rows, features), BF16),
            pltpu.VMEM((features, inner), BF16),
            pltpu.VMEM((half, features), BF16),
            pltpu.VMEM((rows, features), BF16),
            pltpu.SemaphoreType.DMA((halves,)),
            pltpu.SemaphoreType.DMA((steps,)),
            pltpu.SemaphoreType.DMA((steps,)),
            pltpu.SemaphoreType.DMA((groups, halves // 2)),
        ],
        compiler_params=params(),
        cost_estimate=pl.CostEstimate(
            flops=6 * rows * features * half, bytes_accessed=16 * MIB, transcendentals=0
        ),
        name="expert_forward",
    )(*arrays, inward, outward)
    return results[0], results[1], results[2:]


def act_grad_kernel(arrays, places, outward, is_draft):
    count, halves, rows = len(arrays), len(places), len(places) // 2 * arrays[0].shape[0]
    half, features = outward.shape
    chunk = min(CHUNK, features)
    steps = features // chunk

    def body(flag, *refs):
        pl.when(flag[0] == 1)(functools.partial(work, *refs))

    def work(*refs):
        given, w_out, out, s, held_out, s_sems, out_sems = refs[:count], *refs[count:]
        s_copies = row_copies(given, places, s, s_sems)
        start_all(s_copies)
        wait_weight = ahead(weight_copies(w_out, held_out, out_sems, chunk, False))
        wait_all(s_copies)
        act_grad = jnp.zeros((rows, half), F32)
        for c in range(steps):
            wait_weight(c)
            part = columns(c, chunk)
            act_grad = act_grad + dot(s[:, part], held_out[:, part], 1, 1)
        out[...] = act_grad

    return pl.pallas_call(
        body,
        in_specs=[IN_SMEM] + [ANYWHERE] * (count + 1),
        out_specs=IN_VMEM,
        out_shape=jax.ShapeDtypeStruct((rows, half), F32),
        scratch_shapes=[
            pltpu.VMEM((rows, features), BF16),
            pltpu.VMEM((half, features), BF16),
            pltpu.SemaphoreType.DMA((halves,)),
            pltpu.SemaphoreType.DMA((steps,)),
        ],
        compiler_params=params(),
        cost_estimate=pl.CostEstimate(
            flops=2 * rows * features * half, bytes_accessed=8 * MIB, transcendentals=0
        ),
        name="act_grads",
    )(is_draft, *arrays, outward)


def draft_backward_kernel(arrays, places, act_grads, inward, is_draft):
    count, halves, rows = len(arrays), len(places), len(places) // 2 * arrays[0].shape[0]
    features, inner = inward.shape
    half = inner // 2
    chunk = min(CHUNK, features)
    steps = features // chunk
    groups = min(GROUPS, steps)

    def body(flag, *refs):
        pl.when(flag[0] == 1)(functools.partial(work, *refs))
        pl.when(flag[0] != 1)(functools.partial(skip, *refs))

    def skip(*refs):
        (middle, active), refs = refs[count + 2 : count + 4], refs[count + 4 :]
        back, x, done_sems = refs[:-5], refs[-5], refs[-1]
        middle[...] = jnp.zeros_like(middle)
        active[...] = jnp.zeros_like(active)
        size = back[0].shape[0]
        x[:size] = jnp.zeros((size, features), BF16)
        copies = [
            pltpu.make_async_copy(x.at[pl.ds(0, size), :], piece, done_sems.at[0, i])
            for i, piece in enumerate(back)
        ]
        start_all(copies)
        wait_all(copies)

    def work(*refs):
        given, (act_grad, w_in, middle, active), refs = (
            refs[:count], refs[count : count + 4], refs[count + 4 :],
        )
        back, (x, held_in, x_sems, in_sems, done_sems) = refs[:-5], refs[-5:]
        x_copies = row_copies(given, places, x, x_sems)
        start_all(x_copies)
        wait_weight = ahead(weight_copies(w_in, held_in, in_sems, chunk, True))
        wait_all(x_copies)
        total = jnp.zeros((rows, inner), F32)
        for c in range(steps):
            wait_weight(c)
            total = total + dot(x[:, columns(c, chunk)], held_in[columns(c, chunk), :])
        active[...] = activation(total, half)
        middle[...] = middle_grad(total, act_grad[...], half)
        back_rows(middle[...], held_in, x, back, done_sems, chunk, steps)

    results = pl.pallas_call(
        body,
        in_specs=[IN_SMEM] + [ANYWHERE] * count + [IN_VMEM, ANYWHERE],
        out_specs=[IN_VMEM] * 2 + [ANYWHERE] * (halves // 2),
        out_shape=[
            jax.ShapeDtypeStruct((rows, inner), BF16),
            jax.ShapeDtypeStruct((rows, half), BF16),
        ]
        + [jax.ShapeDtypeStruct((2 * rows // halves, features), BF16)] * (halves // 2),
        scratch_shapes=[
            pltpu.VMEM((rows, features), BF16),
            pltpu.VMEM((features, inner), BF16),
            pltpu.SemaphoreType.DMA((halves,)),
            pltpu.SemaphoreType.DMA((steps,)),
            pltpu.SemaphoreType.DMA((groups, halves // 2)),
        ],
        compiler_params=params(),
        cost_estimate=pl.CostEstimate(
            flops=4 * rows * features * inner, bytes_accessed=12 * MIB, transcendentals=0
        ),
        name="draft_backward",
    )(is_draft, *arrays, act_grads, inward)
    return results[0], results[1], results[2:]


def main_backward_kernel(arrays, places, joined, inward, outward):
    count, halves, rows = len(arrays), len(places), len(places) // 2 * arrays[0].shape[0]
    features, inner = inward.shape
    half = outward.shape[0]
    chunk = min(CHUNK, features)
    steps = features // chunk
    groups = min(GROUPS, steps)

    def body(*refs):
        given, (joined, w_in, w_out, middle), refs = (
            refs[:count], refs[count : count + 4], refs[count + 4 :],
        )
        back, (s, held_in, held_out, s_sems, in_sems, out_sems, done_sems) = refs[:-7], refs[-7:]
        s_copies = row_copies(given, places, s, s_sems)
        start_all(s_copies)
        wait_weight = ahead(
            weight_copies(w_out, held_out, out_sems, chunk, False)
            + weight_copies(w_in, held_in, in_sems, chunk, True)
        )
        wait_all(s_copies)
        act_grad = jnp.zeros((rows, half), F32)
        for c in range(steps):
            wait_weight(c)
            part = columns(c, chunk)
            act_grad = act_grad + dot(s[:, part], held_out[:, part], 1, 1)
        middle[...] = middle_grad(joined[...], act_grad, half)
        back_rows(
            middle[...], held_in, s, back, done_sems, chunk, steps, lambda c: wait_weight(steps + c)
        )

    results = pl.pallas_call(
        body,
        in_specs=[ANYWHERE] * count + [IN_VMEM] + [ANYWHERE] * 2,
        out_specs=[IN_VMEM] + [ANYWHERE] * (halves // 2),
        out_shape=[jax.ShapeDtypeStruct((rows, inner), BF16)]
        + [jax.ShapeDtypeStruct((2 * rows // halves, features), BF16)] * (halves // 2),
        scratch_shapes=[
            pltpu.VMEM((rows, features), BF16),
            pltpu.VMEM((features, inner), BF16),
            pltpu.VMEM((half, features), BF16),
            pltpu.SemaphoreType.DMA((halves,)),
            pltpu.SemaphoreType.DMA((steps,)),
            pltpu.SemaphoreType.DMA((steps,)),
            pltpu.SemaphoreType.DMA((groups, halves // 2)),
        ],
        compiler_params=params(),
        cost_estimate=pl.CostEstimate(
            flops=6 * rows * features * half, bytes_accessed=16 * MIB, transcendentals=0
        ),
        name="main_backward",
    )(*arrays, joined, inward, outward)
    return results[0], results[1:]


def weight_grad_kernel(is_draft, first, second, third, places, middles, actives):
    main_places, draft_places = places
    count, halves, rows = len(first), len(main_places), len(main_places) // 2 * first[0].shape[0]
    features = first[0].shape[1]
    inner, half = middles[0].shape[1], actives[0].shape[1]
    chunk = min(CHUNK, features)
    steps = features // chunk

    def body(flag, *refs):
        one, two, three = refs[:count], refs[count : 2 * count], refs[2 * count : 3 * count]
        main_mid, draft_mid, main_act, draft_act, in_grad, out_grad = refs[
            3 * count : 3 * count + 6
        ]
        x, s, mid, act, in_held, out_held, x_sems, s_sems, in_sems, out_sems = refs[3 * count + 6 :]
        draft = flag[0] == 1

        @pl.when(draft)
        def _():
            start_all(row_copies(two, draft_places, x, x_sems) + row_copies(one, draft_places, s, s_sems))
            mid[...] = draft_mid[...]
            act[...] = draft_act[...]

        @pl.when(jnp.logical_not(draft))
        def _():
            start_all(row_copies(one, main_places, x, x_sems) + row_copies(three, main_places, s, s_sems))
            mid[...] = main_mid[...]
            act[...] = main_act[...]

        wait_all(row_copies(one, main_places, x, x_sems))
        in_copies, out_copies = [], []
        for c in range(steps):
            part = columns(c, chunk)
            in_held[part, :] = dot(x[:, part], mid[...], 0, 0).astype(BF16)
            copy = pltpu.make_async_copy(in_held.at[part, :], in_grad.at[0, part, :], in_sems.at[c])
            copy.start()
            in_copies.append(copy)
        wait_all(row_copies(one, main_places, s, s_sems))
        for c in range(steps):
            part = columns(c, chunk)
            out_held[:, part] = dot(act[...], s[:, part], 0, 0).astype(BF16)
            copy = pltpu.make_async_copy(
                out_held.at[:, part], out_grad.at[0, :, part], out_sems.at[c]
            )
            copy.start()
            out_copies.append(copy)
        wait_all(in_copies + out_copies)

    return pl.pallas_call(
        body,
        in_specs=[pl.BlockSpec(memory_space=pltpu.SMEM)]
        + [ANYWHERE] * (3 * count)
        + [IN_VMEM] * 4,
        out_specs=[ANYWHERE] * 2,
        out_shape=[
            jax.ShapeDtypeStruct((1, features, inner), BF16),
            jax.ShapeDtypeStruct((1, half, features), BF16),
        ],
        scratch_shapes=[
            pltpu.VMEM((rows, features), BF16),
            pltpu.VMEM((rows, features), BF16),
            pltpu.VMEM((rows, inner), BF16),
            pltpu.VMEM((rows, half), BF16),
            pltpu.VMEM((features, inner), BF16),
            pltpu.VMEM((half, features), BF16),
            pltpu.SemaphoreType.DMA((halves,)),
            pltpu.SemaphoreType.DMA((halves,)),
            pltpu.SemaphoreType.DMA((steps,)),
            pltpu.SemaphoreType.DMA((steps,)),
        ],
        compiler_params=params(),
        cost_estimate=pl.CostEstimate(
            flops=6 * rows * features * half, bytes_accessed=16 * MIB, transcendentals=0
        ),
        name="weight_grads",
    )(is_draft, *first, *second, *third, *middles, *actives)


def on_device(
    hidden_rows,
    embed_rows,
    gain_hidden,
    gain_embed,
    main_route,
    main_gates,
    draft_route,
    draft_gates,
    draft_cotangent,
    expert_in,
    expert_out,
):
    groups, per_group = SIZES[:2]
    counts = ((groups - 1) * per_group * CAP, groups * per_group * CAP)
    inward = expert_in[0]
    outward = expert_out[0]
    gain_hidden = gain_hidden[None]
    gain_embed = gain_embed[None]
    is_draft = (lax.axis_index("g") == groups - 1).astype(jnp.int32)[None]

    send, mixing, picked_mixing, weight, table = tables(
        main_route.T, main_gates.T, draft_route.T, draft_gates.T, hidden_rows, draft_cotangent,
        counts,
    )
    first, _ = plane_gather(flat(exchange(send)), False)
    joined, main_active, partial = forward_kernel(first, PAIRS, inward, outward)
    main_sum, (picked_hidden, picked_embed, picked_cotangent) = plane_sum(
        partial, False, lambda: pick_kernel(table, hidden_rows, embed_rows, draft_cotangent)
    )
    main_total = exchange(main_sum)

    draft_rows = draft_row_kernel(
        picked_hidden, picked_embed, picked_mixing, weight, main_total, gain_hidden, gain_embed,
        counts,
    )
    second, draft_act_grad = plane_gather(
        flat(exchange(draft_rows)), True, lambda: act_grad_kernel(first, PLAIN, outward, is_draft)
    )
    draft_mid, draft_active, draft_back = draft_backward_kernel(
        second, PLAIN, draft_act_grad, inward, is_draft
    )
    draft_total = exchange(plane_sum_direct(draft_back, True))

    signal = main_signal_kernel(
        picked_hidden, picked_cotangent, picked_mixing, weight, main_total, draft_total,
        gain_hidden, counts,
    )
    third, _ = plane_gather(flat(exchange(signal)), False)
    main_mid, main_back = main_backward_kernel(third, PAIRS, joined, inward, outward)
    token_args = (
        hidden_rows, embed_rows, draft_cotangent, mixing, main_total, draft_total, gain_hidden,
        gain_embed, counts,
    )
    back_sum, (settled_grad, embed_grad) = plane_sum(
        main_back,
        False,
        lambda: token_grad_kernel(*token_args),
        lambda early: token_grad_kernel(*token_args, earlier=early),
    )
    back_total = exchange(back_sum)
    in_grad, out_grad = weight_grad_kernel(
        is_draft, first, second, third, (PAIRS, PLAIN), (main_mid, draft_mid),
        (main_active, draft_active),
    )
    hidden_grad = hidden_grad_kernel(settled_grad, mixing, back_total, counts)
    return (hidden_grad, embed_grad, in_grad, out_grad)


def solution(mesh):
    fine = Mesh(mesh.devices.reshape(SIZES), AXES)
    rows = P(AXES, None)
    blocks = P(AXES, None, None)
    return jax.shard_map(
        on_device,
        mesh=fine,
        in_specs=(rows, rows, P(), P(), rows, rows, rows, rows, rows, blocks, blocks),
        out_specs=(rows, rows, blocks, blocks),
        check_vma=False,
    )
```

```python
import functools
import itertools

import jax
import jax.numpy as jnp
from jax import lax
from jax.experimental import pallas as pl
from jax.experimental.pallas import tpu as pltpu
from jax.sharding import Mesh, PartitionSpec as P

CAP = 2
EPSILON = 1e-06
BF16 = jnp.bfloat16
F32 = jnp.float32
AXES = ("g", "z", "y", "x")
SIZES = (4, 4, 4, 2)
LANES = 128
CHUNK = 1792
MIB = 1024 * 1024
GROUPS = 4
EARLY = 3
IN_VMEM = pl.BlockSpec(memory_space=pltpu.VMEM)
ANYWHERE = pl.BlockSpec(memory_space=pl.ANY)
IN_SMEM = pl.BlockSpec(memory_space=pltpu.SMEM)


def mover(draft_only, dy, dx):
    groups, depth, tall, wide = SIZES

    def number(g, z, y, x):
        return ((g * depth + z) * tall + y) * wide + x

    def target(g, z, y, x):
        if not draft_only or g == groups - 1:
            return number(g, z, (y + dy) % tall, x ^ dx)
        if dx:
            return number(g, (z + 1) % depth, y, x) if g == 1 else number(2 - g, z, y, x ^ 1)
        return number(g ^ 1, z, y, x) if g < 2 else number(g, (z + dy) % depth, y, x)

    places = itertools.product(*map(range, SIZES))
    pairs = [(number(*place), target(*place)) for place in places]
    return lambda values: lax.ppermute(values, AXES, pairs)


def movers(draft_only):
    return mover(draft_only, 1, 0), mover(draft_only, -1, 0), mover(draft_only, 0, 1)


def plane_gather(rows, draft_only, beside=None):
    up, down, cross = movers(draft_only)
    half = rows.shape[0] // 2
    below, above, other = up(rows), down(rows), cross(rows)
    made = None
    if beside is not None:
        (below, above, other), made = lax.optimization_barrier(((below, above, other), beside()))
    far = up(below)
    b_other = other[half:]
    b_other_below, b_other_above = up(b_other), down(b_other)
    a_other_below, a_other_above = cross(below[:half]), cross(above[:half])
    a_other_far, b_other_far = cross(far[:half]), down(b_other_above)
    arrays = [
        rows, below, above, other, far, b_other_below, b_other_above, b_other_far, a_other_below,
        a_other_above, a_other_far,
    ]
    return arrays, made


PLACES = ((0, 0), (-1, 0), (1, 0), (0, 1), (2, 0), (-1, 1), (1, 1), (2, 1))
PLAIN = (
    (0, 0), (0, 1), (1, 0), (1, 1), (2, 0), (2, 1), (3, 0), (3, 1),
    (4, 0), (4, 1), (8, 0), (5, 0), (9, 0), (6, 0), (10, 0), (7, 0),
)
PAIRS = (
    (4, 1), (6, 0), (7, 0), (1, 1), (10, 0), (8, 0), (9, 0), (3, 0),
    (2, 1), (4, 0), (5, 0), (1, 0), (2, 0), (3, 1), (0, 0), (0, 1),
)


def plane_sum_direct(partials, draft_only):
    sent = [
        mover(draft_only, dy, dx)(partial)
        for (dy, dx), partial in reversed(list(zip(PLACES, partials))[1:])
    ]

    def body(*refs):
        total = wide(refs[0][...])
        for ref in refs[1:-1]:
            total = total + wide(ref[...])
        refs[-1][...] = paired(total.astype(BF16))

    size = partials[0].shape[0]
    return adder(body, "sums_direct", [partials[0], *sent], [(size // CAP, CAP)])[0]


def wide(values):
    return values.astype(F32)


def adder(body, name, inputs, results):
    features = inputs[0].shape[1]
    return pl.pallas_call(
        body,
        in_specs=[IN_VMEM] * len(inputs),
        out_specs=[IN_VMEM] * len(results),
        out_shape=[jax.ShapeDtypeStruct((*n, features), BF16) for n in results],
        compiler_params=params(8),
        name=name,
    )(*inputs)


def plane_sum(partials, draft_only, beside, beside_next=None):
    up, down, cross = movers(draft_only)
    up_first, down_first, cross_first = partials
    half = up_first.shape[0] // 2
    low, high = slice(0, half), slice(half, 2 * half)

    def second(up_had, down_had, from_up, from_down, from_cross, up_out, down_out):
        up_out[low] = (wide(up_had[low]) + wide(from_up[low])).astype(BF16)
        up_out[high] = (wide(up_had[high]) + wide(from_cross[low])).astype(BF16)
        down_out[low] = (wide(down_had[low]) + wide(from_down[low])).astype(BF16)
        down_out[high] = (wide(down_had[high]) + wide(from_cross[high])).astype(BF16)

    def third(had, up_one, down_two, up_two, cross_two, a_out, b_out):
        a_out[...] = (wide(had[low]) + wide(cross_two[low]) + wide(up_two[high])).astype(BF16)
        b_out[...] = (wide(had[high]) + wide(up_one[high]) + wide(down_two[low])).astype(BF16)

    def fourth(had, down_one, down_two, up_two, cross_two, a_last, b_last, out):
        a_total = wide(had[low]) + wide(cross_two[high]) + wide(down_two[high]) + wide(a_last[...])
        b_total = wide(had[high]) + wide(down_one[high]) + wide(up_two[low]) + wide(b_last[...])
        out[: half // CAP] = paired(a_total.astype(BF16))
        out[half // CAP :] = paired(b_total.astype(BF16))

    up_one, down_one, cross_one = up(up_first), down(down_first), cross(cross_first)
    (up_one, down_one, cross_one), (rest, made) = lax.optimization_barrier(
        ((up_one, down_one, cross_one), beside())
    )
    cross_second, up_next, down_next, last, own = rest
    up_send, down_send = adder(
        second, "sums_second", [up_next, down_next, up_one, down_one, cross_one], [(2 * half,)] * 2
    )
    up_send, down_send, cross_second = lax.optimization_barrier((up_send, down_send, cross_second))
    up_two, down_two, cross_two = up(up_send), down(down_send), cross(cross_second)
    if beside_next is not None:
        (up_two, down_two, cross_two), made = lax.optimization_barrier(
            ((up_two, down_two, cross_two), beside_next(made))
        )
    a_send, b_send = adder(
        third, "sums_third", [last, up_one, down_two, up_two, cross_two], [(half,)] * 2
    )
    (total,) = adder(
        fourth,
        "sums_fourth",
        [own, down_one, down_two, up_two, cross_two, up(a_send), cross(b_send)],
        [(2 * half // CAP, CAP)],
    )
    return total, made


def exchange(rows):
    return lax.all_to_all(rows, ("g", "z"), 0, 0, tiled=True)


def flat(pairs):
    return pairs.reshape(-1, pairs.shape[-1])


def paired(rows):
    return rows.reshape(-1, CAP, rows.shape[-1])


def params(mebibytes=60):
    return pltpu.CompilerParams(vmem_limit_bytes=mebibytes * MIB)


def dot(left, right, over_left=1, over_right=0):
    return lax.dot_general(
        left, right, (((over_left,), (over_right,)), ((), ())), preferred_element_type=F32
    )


def split_three(values):
    high = values.astype(BF16)
    rest = values - high.astype(F32)
    middle = rest.astype(BF16)
    return (high, middle, (rest - middle.astype(F32)).astype(BF16))


def weighted(mixing, rows):
    parts = jnp.concatenate(split_three(mixing), axis=1)
    return dot(parts, jnp.concatenate([rows] * 3, axis=0))


def inverse_rms(values):
    return lax.rsqrt(jnp.mean(values * values, axis=-1, keepdims=True) + EPSILON)


def norm_backward(values, inverse, scaled):
    mean = jnp.mean(values * scaled, axis=-1, keepdims=True)
    return inverse * scaled - values * (inverse * inverse * inverse * mean)


def tables(main_route, main_gates, draft_route, draft_gates, hidden, cotangent, counts):
    main_slots, slots = counts
    tokens, features = hidden.shape
    chunk = features // 2

    def body(mr, mg, dr, dg, hid, cot, send, mix, picked, weight, table):
        @pl.when(pl.program_id(0) == 0)
        def _():
            slot = lax.broadcasted_iota(jnp.int32, (slots, tokens), 0)
            is_main = slot < main_slots
            label = jnp.where(is_main, slot, slot - main_slots) // CAP
            held = jnp.zeros((slots, tokens), F32)
            gates = jnp.zeros((slots, tokens), F32)
            for k in range(mr.shape[0]):
                one = slice(k, k + 1)
                hit = jnp.where(is_main, mr[one, :], dr[one, :]) == label
                held = jnp.where(hit, 1.0, held)
                gates = jnp.where(hit, jnp.where(is_main, mg[one, :], dg[one, :]), gates)
            row = lax.broadcasted_iota(jnp.int32, (tokens, tokens), 0)
            column = lax.broadcasted_iota(jnp.int32, (tokens, tokens), 1)
            before = jnp.where(row < column, 1.0, 0.0).astype(BF16)
            rank = dot(held.astype(BF16), before)
            kept = (held > 0.5) & (rank == (slot % CAP).astype(F32))
            slot_mixing = jnp.where(kept, gates, 0.0)
            chosen = jnp.where(kept, 1.0, 0.0).astype(BF16)
            spare = jnp.zeros((LANES - slots, tokens), F32)
            mixing = jnp.concatenate([slot_mixing, spare], axis=0).T
            mix[...] = mixing
            table[...] = chosen
            high, middle, low = split_three(mixing)
            picked[...] = dot(chosen, high) + dot(chosen, middle) + dot(chosen, low)
            sums = jnp.sum(slot_mixing, axis=1, keepdims=True)
            weight[...] = jnp.broadcast_to(sums, (slots, LANES))

        chosen = table[...]
        hidden_part = dot(chosen, hid[...])
        cotangent_part = dot(chosen, cot[...])
        slot = lax.broadcasted_iota(jnp.int32, (slots, chunk), 0)
        rows = jnp.where(slot < main_slots, hidden_part, weight[:, :1] * cotangent_part)
        send[...] = paired(rows.astype(BF16))

    whole = pl.BlockSpec(main_route.shape, lambda i: (0, 0))
    wide = pl.BlockSpec((tokens, chunk), lambda i: (0, i))
    slim = pl.BlockSpec((slots // CAP, CAP, chunk), lambda i: (0, 0, i))
    small = jax.ShapeDtypeStruct((slots, LANES), F32)
    small_spec = pl.BlockSpec((slots, LANES), lambda i: (0, 0))
    return pl.pallas_call(
        body,
        grid=(features // chunk,),
        in_specs=[whole] * 4 + [wide] * 2,
        out_specs=[
            slim,
            pl.BlockSpec((tokens, LANES), lambda i: (0, 0)),
            small_spec,
            small_spec,
            pl.BlockSpec((slots, tokens), lambda i: (0, 0)),
        ],
        out_shape=[
            jax.ShapeDtypeStruct((slots // CAP, CAP, features), BF16),
            jax.ShapeDtypeStruct((tokens, LANES), F32),
            small,
            small,
            jax.ShapeDtypeStruct((slots, tokens), BF16),
        ],
        compiler_params=params(),
        name="slot_tables",
    )(main_route, main_gates, draft_route, draft_gates, hidden, cotangent)


def pick_kernel(table, hidden, embed, cotangent):
    slots, tokens = table.shape
    features = hidden.shape[1]
    chunk = features // 2

    def body(table, *refs):
        chosen = table[...]
        for source, out in zip(refs[:3], refs[3:]):
            out[...] = dot(chosen, source[...]).astype(BF16)

    wide = pl.BlockSpec((tokens, chunk), lambda i: (0, i))
    slim = pl.BlockSpec((slots, chunk), lambda i: (0, i))
    return pl.pallas_call(
        body,
        grid=(features // chunk,),
        in_specs=[pl.BlockSpec((slots, tokens), lambda i: (0, 0))] + [wide] * 3,
        out_specs=[slim] * 3,
        out_shape=[jax.ShapeDtypeStruct((slots, features), BF16)] * 3,
        compiler_params=params(),
        cost_estimate=pl.CostEstimate(
            flops=6 * slots * tokens * features, bytes_accessed=8 * MIB, transcendentals=0
        ),
        name="slot_rows",
    )(table, hidden, embed, cotangent)


def lane_part(values, low, high):
    lane = lax.broadcasted_iota(jnp.int32, values.shape, 1)
    return jnp.where((lane >= low) & (lane < high), values, 0.0)


def row_part(values, low, high):
    row = lax.broadcasted_iota(jnp.int32, values.shape, 0)
    return jnp.where((row >= low) & (row < high), values, jnp.zeros_like(values))


def whole(array):
    return pl.BlockSpec(array.shape, lambda i: (0,) * array.ndim)


def draft_row_kernel(hp, ep, picked, weight, main_total, gain_hidden, gain_embed, counts):
    main_slots, slots = counts

    def body(hp, ep, picked, weight, total, gain_h, gain_e, out):
        mixing = lane_part(picked[:, :slots], 0, main_slots)
        settled = hp[...].astype(F32) + weighted(mixing, flat(total[...]))
        embedded = ep[...].astype(F32)
        joined = (
            settled * inverse_rms(settled) * gain_h[...]
            + embedded * inverse_rms(embedded) * gain_e[...]
        )
        joined = jnp.where(weight[:, :1] > 0.0, joined, 0.0)
        out[...] = paired(row_part(joined, main_slots, slots).astype(BF16))

    given = (hp, ep, picked, weight, main_total, gain_hidden, gain_embed)
    return pl.pallas_call(
        body,
        grid=(1,),
        in_specs=[whole(v) for v in given],
        out_specs=whole(main_total),
        out_shape=jax.ShapeDtypeStruct(main_total.shape, BF16),
        compiler_params=params(),
        name="draft_rows",
    )(*given)


def main_signal_kernel(hp, cp, picked, weight, main_total, draft_total, gain_hidden, counts):
    main_slots, slots = counts

    def body(hp, cp, picked, weight, total, drafts, gain_h, out):
        mixing = picked[:, :slots]
        settled = hp[...].astype(F32) + weighted(
            lane_part(mixing, 0, main_slots), flat(total[...])
        )
        lifted = cp[...].astype(F32) + weighted(
            lane_part(mixing, main_slots, slots), flat(drafts[...])
        )
        grad = norm_backward(settled, inverse_rms(settled), gain_h[...] * lifted)
        out[...] = paired(row_part(weight[:, :1] * grad, 0, main_slots).astype(BF16))

    given = (hp, cp, picked, weight, main_total, draft_total, gain_hidden)
    return pl.pallas_call(
        body,
        grid=(1,),
        in_specs=[whole(v) for v in given],
        out_specs=whole(main_total),
        out_shape=jax.ShapeDtypeStruct(main_total.shape, BF16),
        compiler_params=params(),
        name="main_signals",
    )(*given)


def token_grad_kernel(
    hidden, embed, cotangent, mixing, main_total, draft_total, gain_hidden, gain_embed, counts,
    earlier=None,
):
    main_slots, slots = counts
    tokens, features = hidden.shape
    block = 16
    steps = tokens // block // 2
    first = 0 if earlier is None else steps
    held = () if earlier is None else tuple(earlier)

    def body(hid, emb, cot, mix, total, drafts, gain_h, gain_e, *refs):
        settled_grad, embed_grad = refs[-2:]
        mixed = mix[:, :slots]
        settled = hid[...].astype(F32) + weighted(
            lane_part(mixed, 0, main_slots), flat(total[...])
        )
        lifted = cot[...].astype(F32) + weighted(
            lane_part(mixed, main_slots, slots), flat(drafts[...])
        )
        settled_grad[...] = norm_backward(settled, inverse_rms(settled), gain_h[...] * lifted)
        embedded = emb[...].astype(F32)
        embed_grad[...] = norm_backward(
            embedded, inverse_rms(embedded), gain_e[...] * lifted
        ).astype(BF16)

    wide = pl.BlockSpec((block, features), lambda i: (first + i, 0))
    slim = pl.BlockSpec((slots // CAP, CAP, features), lambda i: (0, 0, 0))
    gain = pl.BlockSpec((1, features), lambda i: (0, 0))
    return pl.pallas_call(
        body,
        grid=(steps,),
        in_specs=[wide] * 3
        + [pl.BlockSpec((block, LANES), lambda i: (first + i, 0))]
        + [slim] * 2
        + [gain] * 2
        + [ANYWHERE] * len(held),
        input_output_aliases={8 + k: k for k in range(len(held))},
        out_specs=[wide] * 2,
        out_shape=[
            jax.ShapeDtypeStruct(hidden.shape, F32),
            jax.ShapeDtypeStruct(hidden.shape, BF16),
        ],
        compiler_params=params(),
        cost_estimate=pl.CostEstimate(
            flops=tokens * features * 50, bytes_accessed=6 * tokens * features, transcendentals=0
        ),
        name="token_grads",
    )(hidden, embed, cotangent, mixing, main_total, draft_total, gain_hidden, gain_embed, *held)


def hidden_grad_kernel(settled_grad, mixing, back_total, counts):
    main_slots, slots = counts
    tokens, features = settled_grad.shape
    chunk = features // 2

    def body(grad, mix, total, out):
        mixed = lane_part(mix[:, :slots], 0, main_slots)
        out[...] = (
            grad[...] + weighted(mixed, flat(total[...]))
        ).astype(BF16)

    wide = pl.BlockSpec((tokens, chunk), lambda i: (0, i))
    return pl.pallas_call(
        body,
        grid=(features // chunk,),
        in_specs=[
            wide,
            pl.BlockSpec((tokens, LANES), lambda i: (0, 0)),
            pl.BlockSpec((slots // CAP, CAP, chunk), lambda i: (0, 0, i)),
        ],
        out_specs=wide,
        out_shape=jax.ShapeDtypeStruct(settled_grad.shape, BF16),
        compiler_params=params(),
        name="hidden_grads",
    )(settled_grad, mixing, back_total)


def columns(index, chunk):
    return pl.ds(index * chunk, chunk)


def row_copies(arrays, places, held, sems):
    size = held.shape[0] // len(places)
    return [
        pltpu.make_async_copy(
            arrays[which].at[pl.ds(half * size, size), :],
            held.at[pl.ds(i * size, size), :],
            sems.at[i],
        )
        for i, (which, half) in enumerate(places)
    ]


def weight_copies(whole, held, sems, chunk, over_rows):
    made = []
    for c in range(sems.shape[0]):
        place = (columns(c, chunk), slice(None)) if over_rows else (slice(None), columns(c, chunk))
        made.append(pltpu.make_async_copy(whole.at[place], held.at[place], sems.at[c]))
    return made


def ahead(copies, depth=2):
    start_all(copies[:depth])

    def wait(i):
        copies[i].wait()
        start_all(copies[i + depth : i + depth + 1])

    return wait


def sent_columns(held, pairs, sems, group, chunk, steps):
    size = pairs[0].shape[0]
    first, end = group * steps // sems.shape[0], (group + 1) * steps // sems.shape[0]
    part = pl.ds(first * chunk, (end - first) * chunk)
    return [
        pltpu.make_async_copy(
            held.at[pl.ds(i * size, size), part], pair.at[:, part], sems.at[group, i]
        )
        for i, pair in enumerate(pairs)
    ]


def start_all(copies):
    for copy in copies:
        copy.start()


def wait_all(copies):
    for copy in copies:
        copy.wait()


def activation(joined, half):
    gate, up = joined[:, :half], joined[:, half:]
    return (gate * jax.nn.sigmoid(gate) * up).astype(BF16)


def middle_grad(joined, act_grad, half):
    gate, up = joined[:, :half], joined[:, half:]
    sigmoid_gate = jax.nn.sigmoid(gate)
    gate_grad = act_grad * up * sigmoid_gate * (1.0 + gate * (1.0 - sigmoid_gate))
    up_grad = act_grad * gate * sigmoid_gate
    return jnp.concatenate([gate_grad, up_grad], axis=1).astype(BF16)


def back_rows(mid, held_in, held, back, sems, chunk, steps, before=None):
    groups = sems.shape[0]
    done = []
    for c in range(steps):
        if before is not None:
            before(c)
        part = columns(c, chunk)
        held[: mid.shape[0], part] = dot(mid, held_in[part, :], 1, 1).astype(BF16)
        if (c + 1) * groups // steps > c * groups // steps:
            group = (c + 1) * groups // steps - 1
            copies = sent_columns(held, back, sems, group, chunk, steps)
            start_all(copies)
            done += copies
    wait_all(done)


def forward_kernel(arrays, places, inward, outward):
    count, halves, rows = len(arrays), len(places), len(places) // 2 * arrays[0].shape[0]
    features, inner = inward.shape
    half = outward.shape[0]
    chunk = min(CHUNK, features)
    steps = features // chunk
    groups = min(GROUPS, steps)
    soon = 2 * EARLY * rows // halves

    def body(*refs):
        given, (w_in, w_out), refs = refs[:count], refs[count : count + 2], refs[count + 2 :]
        (joined, active), partial = refs[:2], refs[2 : 2 + EARLY]
        x, held_in, held_out, out, x_sems, in_sems, out_sems, done_sems = refs[2 + EARLY :]
        x_copies = row_copies(given, places, x, x_sems)
        start_all(x_copies)
        wait_weight = ahead(
            weight_copies(w_in, held_in, in_sems, chunk, True)
            + weight_copies(w_out, held_out, out_sems, chunk, False)
        )
        wait_all(x_copies)
        total = jnp.zeros((rows, inner), F32)
        for c in range(steps):
            wait_weight(c)
            total = total + dot(x[:, columns(c, chunk)], held_in[columns(c, chunk), :])
        joined[...] = total
        act = activation(total, half)
        active[...] = act
        done = []
        for c in range(steps):
            wait_weight(steps + c)
            out[:, columns(c, chunk)] = dot(act[:soon], held_out[:, columns(c, chunk)]).astype(BF16)
            if (c + 1) * groups // steps > c * groups // steps:
                group = (c + 1) * groups // steps - 1
                copies = sent_columns(out, partial, done_sems, group, chunk, steps)
                start_all(copies)
                done += copies
        wait_all(done)

    pair = jax.ShapeDtypeStruct((2 * rows // halves, features), BF16)
    results = pl.pallas_call(
        body,
        in_specs=[ANYWHERE] * (count + 2),
        out_specs=[IN_VMEM] * 2 + [ANYWHERE] * EARLY,
        out_shape=[
            jax.ShapeDtypeStruct((rows, inner), F32),
            jax.ShapeDtypeStruct((rows, half), BF16),
        ]
        + [pair] * EARLY,
        scratch_shapes=[
            pltpu.VMEM((rows, features), BF16),
            pltpu.VMEM((features, inner), BF16),
            pltpu.VMEM((half, features), BF16),
            pltpu.VMEM((soon, features), BF16),
            pltpu.SemaphoreType.DMA((halves,)),
            pltpu.SemaphoreType.DMA((steps,)),
            pltpu.SemaphoreType.DMA((steps,)),
            pltpu.SemaphoreType.DMA((groups, EARLY)),
        ],
        compiler_params=params(),
        cost_estimate=pl.CostEstimate(
            flops=6 * rows * features * half, bytes_accessed=16 * MIB, transcendentals=0
        ),
        name="expert_forward",
    )(*arrays, inward, outward)
    return results[0], results[1], results[2:]


def rest_kernel(values, weights, turned, pairs=5):
    rows, inner = values.shape
    features = weights.shape[0] if turned else weights.shape[1]
    size = rows // (EARLY + pairs)
    late = pairs * size
    chunk = min(CHUNK, features)
    steps = features // chunk

    def body(given, whole_weights, *refs):
        back, (held, out, sems, done_sems) = refs[:pairs], refs[pairs:]
        copies = weight_copies(whole_weights, held, sems, chunk, turned)
        start_all(copies)
        left = given[rows - late :, :]
        done = []
        for c in range(steps):
            copies[c].wait()
            part = columns(c, chunk)
            right = held[part, :] if turned else held[:, part]
            out[:, part] = dot(left, right, 1, 1 if turned else 0).astype(BF16)
            made = sent_columns(out, back, done_sems, c, chunk, steps)
            start_all(made)
            done += made
        wait_all(done)

    return pl.pallas_call(
        body,
        in_specs=[IN_VMEM, ANYWHERE],
        out_specs=[ANYWHERE] * pairs,
        out_shape=[jax.ShapeDtypeStruct((size, features), BF16)] * pairs,
        scratch_shapes=[
            pltpu.VMEM(weights.shape, BF16),
            pltpu.VMEM((late, features), BF16),
            pltpu.SemaphoreType.DMA((steps,)),
            pltpu.SemaphoreType.DMA((steps, pairs)),
        ],
        compiler_params=params(),
        cost_estimate=pl.CostEstimate(
            flops=2 * late * inner * features, bytes_accessed=8 * MIB, transcendentals=0
        ),
        name="later_rows",
    )(values, weights)


def act_grad_kernel(arrays, places, outward, is_draft):
    count, halves, rows = len(arrays), len(places), len(places) // 2 * arrays[0].shape[0]
    half, features = outward.shape
    chunk = min(CHUNK, features)
    steps = features // chunk

    def body(flag, *refs):
        pl.when(flag[0] == 1)(functools.partial(work, *refs))

    def work(*refs):
        given, w_out, out, s, held_out, s_sems, out_sems = refs[:count], *refs[count:]
        s_copies = row_copies(given, places, s, s_sems)
        start_all(s_copies)
        wait_weight = ahead(weight_copies(w_out, held_out, out_sems, chunk, False))
        wait_all(s_copies)
        act_grad = jnp.zeros((rows, half), F32)
        for c in range(steps):
            wait_weight(c)
            part = columns(c, chunk)
            act_grad = act_grad + dot(s[:, part], held_out[:, part], 1, 1)
        out[...] = act_grad

    return pl.pallas_call(
        body,
        in_specs=[IN_SMEM] + [ANYWHERE] * (count + 1),
        out_specs=IN_VMEM,
        out_shape=jax.ShapeDtypeStruct((rows, half), F32),
        scratch_shapes=[
            pltpu.VMEM((rows, features), BF16),
            pltpu.VMEM((half, features), BF16),
            pltpu.SemaphoreType.DMA((halves,)),
            pltpu.SemaphoreType.DMA((steps,)),
        ],
        compiler_params=params(),
        cost_estimate=pl.CostEstimate(
            flops=2 * rows * features * half, bytes_accessed=8 * MIB, transcendentals=0
        ),
        name="act_grads",
    )(is_draft, *arrays, outward)


def draft_backward_kernel(arrays, places, act_grads, inward, is_draft):
    count, halves, rows = len(arrays), len(places), len(places) // 2 * arrays[0].shape[0]
    features, inner = inward.shape
    half = inner // 2
    chunk = min(CHUNK, features)
    steps = features // chunk
    groups = min(GROUPS, steps)

    def body(flag, *refs):
        pl.when(flag[0] == 1)(functools.partial(work, *refs))
        pl.when(flag[0] != 1)(functools.partial(skip, *refs))

    def skip(*refs):
        (middle, active), refs = refs[count + 2 : count + 4], refs[count + 4 :]
        back, x, done_sems = refs[:-5], refs[-5], refs[-1]
        middle[...] = jnp.zeros_like(middle)
        active[...] = jnp.zeros_like(active)
        size = back[0].shape[0]
        x[:size] = jnp.zeros((size, features), BF16)
        copies = [
            pltpu.make_async_copy(x.at[pl.ds(0, size), :], piece, done_sems.at[0, i])
            for i, piece in enumerate(back)
        ]
        start_all(copies)
        wait_all(copies)

    def work(*refs):
        given, (act_grad, w_in, middle, active), refs = (
            refs[:count], refs[count : count + 4], refs[count + 4 :],
        )
        back, (x, held_in, x_sems, in_sems, done_sems) = refs[:-5], refs[-5:]
        x_copies = row_copies(given, places, x, x_sems)
        start_all(x_copies)
        wait_weight = ahead(weight_copies(w_in, held_in, in_sems, chunk, True))
        wait_all(x_copies)
        total = jnp.zeros((rows, inner), F32)
        for c in range(steps):
            wait_weight(c)
            total = total + dot(x[:, columns(c, chunk)], held_in[columns(c, chunk), :])
        active[...] = activation(total, half)
        middle[...] = middle_grad(total, act_grad[...], half)
        back_rows(middle[...], held_in, x, back, done_sems, chunk, steps)

    results = pl.pallas_call(
        body,
        in_specs=[IN_SMEM] + [ANYWHERE] * count + [IN_VMEM, ANYWHERE],
        out_specs=[IN_VMEM] * 2 + [ANYWHERE] * (halves // 2),
        out_shape=[
            jax.ShapeDtypeStruct((rows, inner), BF16),
            jax.ShapeDtypeStruct((rows, half), BF16),
        ]
        + [jax.ShapeDtypeStruct((2 * rows // halves, features), BF16)] * (halves // 2),
        scratch_shapes=[
            pltpu.VMEM((rows, features), BF16),
            pltpu.VMEM((features, inner), BF16),
            pltpu.SemaphoreType.DMA((halves,)),
            pltpu.SemaphoreType.DMA((steps,)),
            pltpu.SemaphoreType.DMA((groups, halves // 2)),
        ],
        compiler_params=params(),
        cost_estimate=pl.CostEstimate(
            flops=4 * rows * features * inner, bytes_accessed=12 * MIB, transcendentals=0
        ),
        name="draft_backward",
    )(is_draft, *arrays, act_grads, inward)
    return results[0], results[1], results[2:]


def main_backward_kernel(arrays, places, joined, inward, outward):
    count, halves, rows = len(arrays), len(places), len(places) // 2 * arrays[0].shape[0]
    features, inner = inward.shape
    half = outward.shape[0]
    chunk = min(CHUNK, features)
    steps = features // chunk
    groups = min(GROUPS, steps)
    soon = 2 * EARLY * rows // halves

    def body(*refs):
        given, (joined, w_in, w_out, middle), refs = (
            refs[:count], refs[count : count + 4], refs[count + 4 :],
        )
        back, (s, held_in, held_out, s_sems, in_sems, out_sems, done_sems) = refs[:-7], refs[-7:]
        s_copies = row_copies(given, places, s, s_sems)
        start_all(s_copies)
        wait_weight = ahead(
            weight_copies(w_out, held_out, out_sems, chunk, False)
            + weight_copies(w_in, held_in, in_sems, chunk, True)
        )
        wait_all(s_copies)
        act_grad = jnp.zeros((rows, half), F32)
        for c in range(steps):
            wait_weight(c)
            part = columns(c, chunk)
            act_grad = act_grad + dot(s[:, part], held_out[:, part], 1, 1)
        middle[...] = middle_grad(joined[...], act_grad, half)
        back_rows(
            middle[:soon, :], held_in, s, back, done_sems, chunk, steps, lambda c: wait_weight(steps + c)
        )

    results = pl.pallas_call(
        body,
        in_specs=[ANYWHERE] * count + [IN_VMEM] + [ANYWHERE] * 2,
        out_specs=[IN_VMEM] + [ANYWHERE] * EARLY,
        out_shape=[jax.ShapeDtypeStruct((rows, inner), BF16)]
        + [jax.ShapeDtypeStruct((2 * rows // halves, features), BF16)] * EARLY,
        scratch_shapes=[
            pltpu.VMEM((rows, features), BF16),
            pltpu.VMEM((features, inner), BF16),
            pltpu.VMEM((half, features), BF16),
            pltpu.SemaphoreType.DMA((halves,)),
            pltpu.SemaphoreType.DMA((steps,)),
            pltpu.SemaphoreType.DMA((steps,)),
            pltpu.SemaphoreType.DMA((groups, EARLY)),
        ],
        compiler_params=params(),
        cost_estimate=pl.CostEstimate(
            flops=6 * rows * features * half, bytes_accessed=16 * MIB, transcendentals=0
        ),
        name="main_backward",
    )(*arrays, joined, inward, outward)
    return results[0], results[1:]


def weight_grad_kernel(is_draft, first, second, third, places, middles, actives):
    main_places, draft_places = places
    count, halves, rows = len(first), len(main_places), len(main_places) // 2 * first[0].shape[0]
    features = first[0].shape[1]
    inner, half = middles[0].shape[1], actives[0].shape[1]
    chunk = min(CHUNK, features)
    steps = features // chunk

    def body(flag, *refs):
        one, two, three = refs[:count], refs[count : 2 * count], refs[2 * count : 3 * count]
        main_mid, draft_mid, main_act, draft_act, in_grad, out_grad = refs[
            3 * count : 3 * count + 6
        ]
        x, s, mid, act, in_held, out_held, x_sems, s_sems, in_sems, out_sems = refs[3 * count + 6 :]
        draft = flag[0] == 1

        @pl.when(draft)
        def _():
            start_all(row_copies(two, draft_places, x, x_sems) + row_copies(one, draft_places, s, s_sems))
            mid[...] = draft_mid[...]
            act[...] = draft_act[...]

        @pl.when(jnp.logical_not(draft))
        def _():
            start_all(row_copies(one, main_places, x, x_sems) + row_copies(three, main_places, s, s_sems))
            mid[...] = main_mid[...]
            act[...] = main_act[...]

        wait_all(row_copies(one, main_places, x, x_sems))
        in_copies, out_copies = [], []
        for c in range(steps):
            part = columns(c, chunk)
            in_held[part, :] = dot(x[:, part], mid[...], 0, 0).astype(BF16)
            copy = pltpu.make_async_copy(in_held.at[part, :], in_grad.at[0, part, :], in_sems.at[c])
            copy.start()
            in_copies.append(copy)
        wait_all(row_copies(one, main_places, s, s_sems))
        for c in range(steps):
            part = columns(c, chunk)
            out_held[:, part] = dot(act[...], s[:, part], 0, 0).astype(BF16)
            copy = pltpu.make_async_copy(
                out_held.at[:, part], out_grad.at[0, :, part], out_sems.at[c]
            )
            copy.start()
            out_copies.append(copy)
        wait_all(in_copies + out_copies)

    return pl.pallas_call(
        body,
        in_specs=[pl.BlockSpec(memory_space=pltpu.SMEM)]
        + [ANYWHERE] * (3 * count)
        + [IN_VMEM] * 4,
        out_specs=[ANYWHERE] * 2,
        out_shape=[
            jax.ShapeDtypeStruct((1, features, inner), BF16),
            jax.ShapeDtypeStruct((1, half, features), BF16),
        ],
        scratch_shapes=[
            pltpu.VMEM((rows, features), BF16),
            pltpu.VMEM((rows, features), BF16),
            pltpu.VMEM((rows, inner), BF16),
            pltpu.VMEM((rows, half), BF16),
            pltpu.VMEM((features, inner), BF16),
            pltpu.VMEM((half, features), BF16),
            pltpu.SemaphoreType.DMA((halves,)),
            pltpu.SemaphoreType.DMA((halves,)),
            pltpu.SemaphoreType.DMA((steps,)),
            pltpu.SemaphoreType.DMA((steps,)),
        ],
        compiler_params=params(),
        cost_estimate=pl.CostEstimate(
            flops=6 * rows * features * half, bytes_accessed=16 * MIB, transcendentals=0
        ),
        name="weight_grads",
    )(is_draft, *first, *second, *third, *middles, *actives)


def on_device(
    hidden_rows,
    embed_rows,
    gain_hidden,
    gain_embed,
    main_route,
    main_gates,
    draft_route,
    draft_gates,
    draft_cotangent,
    expert_in,
    expert_out,
):
    groups, per_group = SIZES[:2]
    counts = ((groups - 1) * per_group * CAP, groups * per_group * CAP)
    inward = expert_in[0]
    outward = expert_out[0]
    gain_hidden = gain_hidden[None]
    gain_embed = gain_embed[None]
    is_draft = (lax.axis_index("g") == groups - 1).astype(jnp.int32)[None]

    send, mixing, picked_mixing, weight, table = tables(
        main_route.T, main_gates.T, draft_route.T, draft_gates.T, hidden_rows, draft_cotangent,
        counts,
    )
    first, _ = plane_gather(flat(exchange(send)), False)
    joined, main_active, partial = forward_kernel(first, PAIRS, inward, outward)
    main_sum, (picked_hidden, picked_embed, picked_cotangent) = plane_sum(
        partial,
        False,
        lambda: (
            rest_kernel(main_active, outward, False),
            pick_kernel(table, hidden_rows, embed_rows, draft_cotangent),
        ),
    )
    main_total = exchange(main_sum)

    draft_rows = draft_row_kernel(
        picked_hidden, picked_embed, picked_mixing, weight, main_total, gain_hidden, gain_embed,
        counts,
    )
    second, draft_act_grad = plane_gather(
        flat(exchange(draft_rows)), True, lambda: act_grad_kernel(first, PLAIN, outward, is_draft)
    )
    draft_mid, draft_active, draft_back = draft_backward_kernel(
        second, PLAIN, draft_act_grad, inward, is_draft
    )
    draft_total = exchange(plane_sum_direct(draft_back, True))

    signal = main_signal_kernel(
        picked_hidden, picked_cotangent, picked_mixing, weight, main_total, draft_total,
        gain_hidden, counts,
    )
    token_args = (
        hidden_rows, embed_rows, draft_cotangent, mixing, main_total, draft_total, gain_hidden,
        gain_embed, counts,
    )
    third, early = plane_gather(
        flat(exchange(signal)), False, lambda: token_grad_kernel(*token_args)
    )
    main_mid, main_back = main_backward_kernel(third, PAIRS, joined, inward, outward)
    back_sum, (settled_grad, embed_grad) = plane_sum(
        main_back,
        False,
        lambda: (rest_kernel(main_mid, inward, True), early),
        lambda early: token_grad_kernel(*token_args, earlier=early),
    )
    back_total = exchange(back_sum)
    in_grad, out_grad = weight_grad_kernel(
        is_draft, first, second, third, (PAIRS, PLAIN), (main_mid, draft_mid),
        (main_active, draft_active),
    )
    hidden_grad = hidden_grad_kernel(settled_grad, mixing, back_total, counts)
    return (hidden_grad, embed_grad, in_grad, out_grad)


def solution(mesh):
    fine = Mesh(mesh.devices.reshape(SIZES), AXES)
    rows = P(AXES, None)
    blocks = P(AXES, None, None)
    return jax.shard_map(
        on_device,
        mesh=fine,
        in_specs=(rows, rows, P(), P(), rows, rows, rows, rows, rows, blocks, blocks),
        out_specs=(rows, rows, blocks, blocks),
        check_vma=False,
    )
```
